128 devices in a mesh: dp: 8 (over z, core), enc: 16 (over x, y).
Axes of the slice: x: 4, y: 4, z: 4, core: 2. Of those that a mesh axis runs over, the one named last changes fastest.
Arguments:
- queries_in: bfloat16 [4096, 4096], P('dp'), may hold values from -6 to 6
- w_query: bfloat16 [4096, 4096], P(None, 'enc'), may hold values from -0.09375 to 0.09375
- w_key: bfloat16 [896, 4096], P(None, 'enc'), may hold values from -0.1875 to 0.1875
- w_value: bfloat16 [896, 4096], P(None, 'enc'), may hold values from -0.1875 to 0.1875
- tiles: bfloat16 [512, 128, 896], P(('dp', 'enc')), may hold values from -6 to 6
- neighbour_owner: int32 [64, 2], P('dp'), may hold values from 0 to 15, all different within a row; in each aligned block of 8 rows (0 to 7, 8 to 15, ...) at most 2 rows name the same one
- neighbour_slot: int32 [64, 2], P('dp'), may hold values from 0 to 3
- key_length: int32 [64, 2], P('dp'), may hold values from 64 to 128
- grad_context: bfloat16 [4096, 4096], P('dp', 'enc'), may hold values from -6 to 6
Outputs:
- context: bfloat16 [4096, 4096], P('dp', 'enc')
- grad_wq: float32 [4096, 4096], P(None, 'enc')
- grad_wk: float32 [896, 4096], P(None, 'enc')
- grad_wv: float32 [896, 4096], P(None, 'enc')
- grad_tiles: float32 [512, 128, 896], P(('dp', 'enc'))
The draws below stay inside these ranges and needn't reach their ends.
Inputs may be any that keep to these rules, and one draw needn't show every extreme that they name: `neighbour_owner`: within each block of 8 spans (one dp group), no owner is named by more than 2 neighbours, and the 2 owners of one span differ.
All inputs are finite; a program needn't handle non-finite values.
Results may differ from the reference program's by a relative error of at most 0.02.
Values may be sent and summed in bfloat16 or wider, within the bound.
No kernel may reach another device: no remote copies, remote signals or barrier semaphores. Data moves between devices by JAX's collectives and lax.ppermute only.
A program may use at most 128 MiB of HBM per device.

```python
import math
import jax
import jax.numpy as jnp
import numpy as np
from jax import lax

D = 4096
H = 32
DE = 896
HD = 128
SPAN = 64
NTOK = 128
NEIGH = 2
CH_DP = 8
TILE_DEV = 4
CAP = 2
SPANS = 64
TOK = 4096
TILES = 512
N_ENC = 16


def with_ends(entries, stream_key, low, largest):
    dims = entries.shape
    place = [jax.random.randint(jax.random.fold_in(stream_key, axis), (), 0, dims[axis]) for axis in range(len(dims))]
    entries = entries.at[tuple(place)].set(low)
    longest = dims.index(max(dims))
    place[longest] = (place[longest] + 1) % dims[longest]
    return entries.at[tuple(place)].set(largest)


def steps_of(rng, shape, shards, least, largest):
    loudness = 1.0
    for dim, blocks in shards:
        heights = jax.random.uniform(jax.random.fold_in(jax.random.fold_in(rng, 6), dim), (blocks,), jnp.float32, least / len(shards), largest / len(shards))
        loudness = loudness * jnp.repeat(jnp.exp(heights), shape[dim] // blocks).reshape((-1,) + (1,) * (len(shape) - 1 - dim))
    return loudness


def rank_table(number_of, lean):
    loads = [(1 << 20) // math.isqrt(grade ** lean) + 1 for grade in range(1, number_of + 1)]
    width = 1 + sum(loads) // (1 << 30)
    return np.cumsum(np.array([max(1, weight // width) for weight in loads]))


def ranked_ids(stream_key, extent, count, lean):
    listing = rank_table(count, lean)
    ticket = jax.random.randint(jax.random.fold_in(stream_key, 1), extent, 0, int(listing[count - 1]))
    grade = jnp.searchsorted(jnp.asarray(listing, jnp.int32), ticket, side="right")
    return jax.random.permutation(jax.random.fold_in(stream_key, 2), count)[grade].astype(jnp.int32)


def shared_out(stream_key, own, number, rows, amount, top, limit, lean):
    sequence = jax.random.permutation(stream_key, amount)
    packed, ordinary = shares(amount, rows * top, limit, lean, True), shares(amount, rows * top, limit, lean, False)
    places = jnp.arange(amount)

    def named(sizes, turn):
        used = int((sizes > 0).sum())
        fixed = max(1, used // 4)
        moved = fixed + (places - fixed + turn * (used - fixed)) % max(1, amount - fixed)
        return jnp.zeros((amount,), jnp.int32).at[sequence[jnp.where(places < fixed, places, moved)]].set(jnp.asarray(sizes, jnp.int32))

    sizes = jnp.where(number % 4 == 0, named(packed, number // 4), named(ordinary, number - number // 4 - 1))
    mixed = jax.random.permutation(jax.random.fold_in(own, 3), amount)
    giver, taker = mixed[0:amount // 2 * 2:2], mixed[1:amount // 2 * 2:2]
    room = jnp.minimum(sizes[giver] - 1, limit - sizes[taker]) // 2
    room = jnp.where((giver == sequence[0]) | (taker == sequence[0]) | (sizes[taker] == 0), 0, jnp.maximum(room, 0))
    moved = jax.random.randint(jax.random.fold_in(own, 4), (amount // 2,), 0, 1 << 20) % (room + 1)
    sizes = sizes.at[giver].add(-moved).at[taker].add(moved)
    labels = jnp.searchsorted(jnp.cumsum(sizes), jnp.arange(rows * top), side="right").astype(jnp.int32)
    listing = labels.reshape(top, rows).T
    listing = listing[jax.random.permutation(jax.random.fold_in(own, 1), rows)]
    turn = jax.random.randint(jax.random.fold_in(own, 2), (rows, 1), 0, top)
    return jnp.take_along_axis(listing, (jnp.arange(top)[None, :] + turn) % top, axis=1)


def shares(number_of, total, reach, lean, full):
    loads = [(1 << 20) // math.isqrt(rank ** lean) + 1 for rank in range(1, number_of + 1)]
    largest = reach if full else min(reach, max(-(-total // number_of), total * loads[0] // sum(loads)))
    least = 1 if total - largest >= number_of - 1 else 0
    counts, rest = [largest] + [least] * (number_of - 1), total - largest - least * (number_of - 1)
    while rest > 0:
        candidates = [i for i in range(1, number_of) if counts[i] < largest] or [i for i in range(1, number_of) if counts[i] < reach]
        mass, budget = sum([loads[i] for i in candidates]), rest
        for i in candidates:
            addition = min(reach - counts[i], max(1, budget * loads[i] // mass), rest)
            counts[i] = counts[i] + addition
            rest = rest - addition
    return np.array(counts)


def noise(own_key, dims, width, bound, split=(), kind=jnp.bfloat16):
    gain = steps_of(own_key, dims, split, -0.22, 0.18) if split else 1.0
    values = jax.random.normal(own_key, dims, jnp.float32) * width * gain
    return jnp.minimum(jnp.maximum(values, -bound), bound).astype(kind)


def setup_inputs(seed: int = 0) -> dict:
    streams_of = jax.random.split(jax.random.key(seed), 10)
    queries_in = noise(streams_of[0], (TOK, D), 1.0, 6.0, ((0, 8),))
    w_query = noise(streams_of[1], (D, H * HD), D ** -0.5, 0.09375, ((1, 16),))
    w_key = noise(streams_of[2], (DE, H * HD), DE ** -0.5, 0.1875, ((1, 16),))
    w_value = noise(streams_of[3], (DE, H * HD), DE ** -0.5, 0.1875, ((1, 16),))
    tiles = noise(streams_of[4], (TILES, NTOK, DE), 1.0, 6.0, ((0, 128),))
    neighbour_owner_keys = jax.random.split(jax.random.fold_in(streams_of[5], 1), SPANS // CH_DP)
    neighbour_owner_turns = jax.random.permutation(jax.random.fold_in(streams_of[5], 3), SPANS // CH_DP)
    neighbour_owner = jax.vmap(lambda own, number: shared_out(jax.random.fold_in(streams_of[5], 2), own, number, CH_DP, N_ENC, NEIGH, CAP, 2))(neighbour_owner_keys, neighbour_owner_turns).reshape((SPANS, NEIGH))
    neighbour_slot = with_ends(ranked_ids(streams_of[6], (SPANS, NEIGH), TILE_DEV, 2), jax.random.fold_in(streams_of[6], 3), 0, TILE_DEV - 1).astype(jnp.int32)
    key_length = with_ends(jax.random.randint(streams_of[7], (SPANS, NEIGH), NTOK // 2, NTOK + 1), jax.random.fold_in(streams_of[7], 1), NTOK // 2, NTOK).astype(jnp.int32)
    grad_context = noise(streams_of[8], (TOK, H * HD), 1.0, 6.0, ((0, 8), (1, 16)))
    return {"queries_in": queries_in, "w_query": w_query, "w_key": w_key, "w_value": w_value, "tiles": tiles, "neighbour_owner": neighbour_owner, "neighbour_slot": neighbour_slot, "key_length": key_length, "grad_context": grad_context}


def reference(queries_in, w_query, w_key, w_value, tiles, neighbour_owner, neighbour_slot, key_length, grad_context):
    score_scale = 1.0 / (HD ** 0.5)
    head_columns = H * HD
    query = jnp.dot(queries_in, w_query, preferred_element_type=jnp.float32).astype(jnp.bfloat16)
    group_of = (jnp.arange(SPANS, dtype=jnp.int32) // CH_DP)[:, None]
    tile_index = (group_of * (N_ENC * TILE_DEV) + neighbour_owner * TILE_DEV + neighbour_slot).astype(jnp.int32)
    neighbours = tiles[tile_index.reshape(-1)].reshape(SPANS * NEIGH * NTOK, DE)
    key_rows = jnp.dot(neighbours, w_key, preferred_element_type=jnp.float32).astype(jnp.bfloat16)
    value_rows = jnp.dot(neighbours, w_value, preferred_element_type=jnp.float32).astype(jnp.bfloat16)
    query_heads = query.reshape(SPANS, SPAN, H, HD).astype(jnp.float32)
    key_heads = key_rows.reshape(SPANS, NEIGH * NTOK, H, HD).astype(jnp.float32)
    value_heads = value_rows.reshape(SPANS, NEIGH * NTOK, H, HD).astype(jnp.float32)
    score = jnp.einsum("ctha,cnha->chtn", query_heads, key_heads) * score_scale
    position = jnp.arange(NEIGH * NTOK, dtype=jnp.int32) % NTOK
    lengths = jnp.repeat(key_length, NTOK, axis=1)
    visible = (position[None, :] < lengths).astype(jnp.float32)
    weights = jnp.exp(score) * visible[:, None, None, :]
    attention = weights / jnp.sum(weights, axis=-1, keepdims=True)
    attention_b = attention.astype(jnp.bfloat16)
    context = jnp.einsum("chtn,cnha->ctha", attention_b.astype(jnp.float32), value_heads)
    context = context.reshape(TOK, head_columns).astype(jnp.bfloat16)
    upstream = grad_context.reshape(SPANS, SPAN, H, HD).astype(jnp.float32)
    dprobs = jnp.einsum("ctha,cnha->chtn", upstream, value_heads)
    dscore = (attention * (dprobs - jnp.sum(attention * dprobs, axis=-1, keepdims=True)) * score_scale).astype(jnp.bfloat16)
    dscore_f = dscore.astype(jnp.float32)
    query_grad = jnp.einsum("chtn,cnha->ctha", dscore_f, key_heads).reshape(TOK, head_columns).astype(jnp.bfloat16)
    key_grad = jnp.einsum("chtn,ctha->cnha", dscore_f, query_heads).reshape(-1, head_columns).astype(jnp.bfloat16)
    value_grad = jnp.einsum("chtn,ctha->cnha", attention_b.astype(jnp.float32), upstream).reshape(-1, head_columns).astype(jnp.bfloat16)
    grad_wq = jnp.dot(queries_in.T, query_grad, preferred_element_type=jnp.float32)
    grad_wk = jnp.dot(neighbours.T, key_grad, preferred_element_type=jnp.float32)
    grad_wv = jnp.dot(neighbours.T, value_grad, preferred_element_type=jnp.float32)
    group_width = head_columns // N_ENC
    neighbour_grad = jnp.zeros((SPANS * NEIGH * NTOK, DE), jnp.float32)
    for group in range(N_ENC):
        low = group * group_width
        high = low + group_width
        term = jnp.dot(key_grad[:, low:high], w_key[:, low:high].T, preferred_element_type=jnp.float32)
        term = term + jnp.dot(value_grad[:, low:high], w_value[:, low:high].T, preferred_element_type=jnp.float32)
        rounded = lax.optimization_barrier(term.astype(jnp.bfloat16))
        neighbour_grad = neighbour_grad + rounded.astype(jnp.float32)
    grad_tiles = jnp.zeros((TILES, NTOK, DE), jnp.float32).at[tile_index.reshape(-1)].add(
        neighbour_grad.reshape(SPANS * NEIGH, NTOK, DE))
    return context, grad_wq, grad_wk, grad_wv, grad_tiles
```

```python
import jax
import jax.numpy as jnp
from jax import lax
from jax.experimental import pallas as pl
from jax.experimental.pallas import tpu as pltpu
from jax.sharding import PartitionSpec as P

HD = 128
SPAN = 64
SIDE = 4
SUB = 16
NT = 16
VMEM_LIMIT = 48 * 1024 * 1024
F32 = jnp.float32
BF16 = jnp.bfloat16


def along_x(value, step):
    pairs = [(i, ((i // SIDE + step) % SIDE) * SIDE + i % SIDE) for i in range(SIDE * SIDE)]
    return lax.ppermute(value, "enc", pairs)


def along_y(value, step):
    pairs = [(i, (i // SIDE) * SIDE + (i + step) % SIDE) for i in range(SIDE * SIDE)]
    return lax.ppermute(value, "enc", pairs)


def place():
    own = lax.axis_index("enc")
    return own, lax.div(own, SIDE), lax.rem(own, SIDE)


def apart(here, there):
    return lax.rem(here - there + SIDE, SIDE)


def my_slots(owner, slot, own):
    count = jnp.int32(0)
    first = jnp.int32(0)
    second = jnp.int32(0)
    for t in range(NT):
        hit = owner[t // 2, t % 2] == own
        tile = slot[t // 2, t % 2]
        first = jnp.where(hit & (count == 0), tile, first)
        second = jnp.where(hit & (count == 1), tile, second)
        count = count + hit.astype(jnp.int32)
    return first, second


def named(owner, x, y):
    found = []
    for t in range(NT):
        o = owner[t // 2, t % 2]
        rank = jnp.int32(0)
        for e in range(t):
            rank = rank + (owner[e // 2, e % 2] == o).astype(jnp.int32)
        found.append((apart(x, lax.div(o, SIDE)), apart(y, lax.rem(o, SIDE)), rank))
    return found


def sub_row(at, base):
    return pl.ds(pl.multiple_of(base + lax.rem(at, SIDE) * SUB, SUB), SUB)


def split_kernel(owner, slot, tiles, *outs):
    own, x, y = place()
    for r, tile in enumerate(my_slots(owner, slot, own)):
        for k in range(SIDE):
            outs[k][r] = tiles[tile, sub_row(x + k, 0), :]
            outs[SIDE + k][r] = tiles[tile, sub_row(y + k, SIDE * SUB), :]


def compact_kernel(owner, *refs):
    in_a, in_b = refs[:SIDE], refs[SIDE : 2 * SIDE]
    out_a, out_b = refs[2 * SIDE :]
    _, x, y = place()
    for t, (dx, dy, rank) in enumerate(named(owner, x, y)):
        for step in range(SIDE):

            @pl.when(dy == step)
            def _(t=t, step=step, at=dx * 2 + rank):
                out_a[t] = in_a[step][at]

            @pl.when(dx == step)
            def _(t=t, step=step, at=dy * 2 + rank):
                out_b[t] = in_b[step][at]


def expand_kernel(owner, *refs):
    in_a, in_b = refs[:SIDE], refs[SIDE : 2 * SIDE]
    out_a, out_b = refs[2 * SIDE : 3 * SIDE], refs[3 * SIDE :]
    _, x, y = place()
    for out in out_a + out_b:
        out[...] = jnp.zeros_like(out)
    for t, (dx, dy, rank) in enumerate(named(owner, x, y)):
        total_a = sum(ref[t].astype(F32) for ref in in_a).astype(BF16)
        total_b = sum(ref[t].astype(F32) for ref in in_b).astype(BF16)
        for step in range(SIDE):

            @pl.when(dy == step)
            def _(step=step, at=dx * 2 + rank, total=total_a):
                out_a[step][at] = total

            @pl.when(dx == step)
            def _(step=step, at=dy * 2 + rank, total=total_b):
                out_b[step][at] = total


def owners_sum_kernel(*refs):
    in_a, in_b = refs[:SIDE], refs[SIDE : 2 * SIDE]
    out_a, out_b = refs[2 * SIDE : 3 * SIDE], refs[3 * SIDE :]
    for ins, outs in ((in_a, out_a), (in_b, out_b)):
        for k in range(SIDE):
            for r in range(2):
                outs[k][r] = sum(ref[k * 2 + r].astype(F32) for ref in ins).astype(BF16)


def tiles_kernel(owner, slot, *refs):
    in_a, in_b, out = refs[:SIDE], refs[SIDE : 2 * SIDE], refs[2 * SIDE]
    own, x, y = place()
    out[...] = jnp.zeros_like(out)
    for r, tile in enumerate(my_slots(owner, slot, own)):
        for k in range(SIDE):
            out[tile, sub_row(x + k, 0), :] += in_a[k][r].astype(F32)
            out[tile, sub_row(y + k, SIDE * SUB), :] += in_b[k][r].astype(F32)


def dot(a, b, a_dim, b_dim):
    return lax.dot_general(a, b, (((a_dim,), (b_dim,)), ((), ())), preferred_element_type=F32)


def attention_kernel(length, *refs):
    in_a, in_b = refs[:SIDE], refs[SIDE : 2 * SIDE]
    q_ref, up_ref, wk_ref, wv_ref = refs[8:12]
    ctx_ref, qg_ref = refs[12:14]
    out_a, out_b = refs[14:18], refs[18:22]
    gwk_ref, gwv_ref = refs[22:24]
    acc_k, acc_v = refs[24:26]
    span = pl.program_id(0)
    _, x, y = place()
    rows = [ref[j] for j in range(2) for ref in in_a + in_b]
    near = jnp.concatenate(rows, axis=0)
    key = dot(near, wk_ref[...], 1, 0).astype(BF16)
    value = dot(near, wv_ref[...], 1, 0).astype(BF16)
    row = lax.broadcasted_iota(jnp.int32, (1, 2 * 2 * SIDE * SUB), 1)
    lower = (row // (SIDE * SUB)) % 2
    block = (jnp.where(lower == 0, x, y) - (row // SUB) % SIDE + SIDE) % SIDE
    position = lower * (SIDE * SUB) + block * SUB + row % SUB
    limit = jnp.where(row < 2 * SIDE * SUB, length[span, 0], length[span, 1])
    visible = position < limit
    scale = 1.0 / HD**0.5
    key_grads = []
    value_grads = []
    for h in range(q_ref.shape[1] // HD):
        cols = slice(h * HD, (h + 1) * HD)
        q = q_ref[:, cols]
        up = up_ref[:, cols]
        key_h = key[:, cols]
        value_h = value[:, cols]
        score = dot(q, key_h, 1, 1) * scale
        weights = jnp.where(visible, jnp.exp(score), 0.0)
        attention = weights / jnp.sum(weights, axis=-1, keepdims=True)
        attention_b = attention.astype(BF16)
        ctx_ref[:, cols] = dot(attention_b, value_h, 1, 0).astype(BF16)
        dprobs = dot(up, value_h, 1, 1)
        inner = jnp.sum(attention * dprobs, axis=-1, keepdims=True)
        dscore = (attention * (dprobs - inner) * scale).astype(BF16)
        qg_ref[:, cols] = dot(dscore, key_h, 1, 0).astype(BF16)
        key_grads.append(dot(dscore, q, 0, 0).astype(BF16))
        value_grads.append(dot(attention_b, up, 0, 0).astype(BF16))
    key_grad = jnp.concatenate(key_grads, axis=1)
    value_grad = jnp.concatenate(value_grads, axis=1)
    partial = dot(key_grad, wk_ref[...], 1, 1) + dot(value_grad, wv_ref[...], 1, 1)
    partial = partial.astype(BF16)
    for j in range(2):
        for k, out in enumerate(out_a + out_b):
            low = (j * 2 * SIDE + k) * SUB
            out[j] = partial[low : low + SUB]
    step_k = dot(near, key_grad, 0, 0)
    step_v = dot(near, value_grad, 0, 0)

    @pl.when(span == 0)
    def _():
        acc_k[...] = step_k
        acc_v[...] = step_v

    @pl.when(span > 0)
    def _():
        acc_k[...] += step_k
        acc_v[...] += step_v

    @pl.when(span == pl.num_programs(0) - 1)
    def _():
        gwk_ref[...] = acc_k[...].astype(BF16)
        gwv_ref[...] = acc_v[...].astype(BF16)


def call(kernel, scalars, ins, outs):
    vmem = pl.BlockSpec(memory_space=pltpu.VMEM)
    return pl.pallas_call(
        kernel,
        out_shape=[jax.ShapeDtypeStruct(shape, dtype) for shape, dtype in outs],
        in_specs=[pl.BlockSpec(memory_space=pltpu.SMEM)] * len(scalars) + [vmem] * len(ins),
        out_specs=[vmem] * len(outs),
        compiler_params=pltpu.CompilerParams(vmem_limit_bytes=VMEM_LIMIT),
    )(*scalars, *ins)


def attend(key_length, parts, query, upstream, w_key, w_value):
    spans = key_length.shape[0]
    width, columns = w_key.shape
    tile_block = pl.BlockSpec((2, SUB, width), lambda c, *_: (c, 0, 0))
    token_block = pl.BlockSpec((SPAN, columns), lambda c, *_: (c, 0))
    whole = pl.BlockSpec((width, columns), lambda c, *_: (0, 0))
    return pl.pallas_call(
        attention_kernel,
        grid_spec=pltpu.PrefetchScalarGridSpec(
            num_scalar_prefetch=1,
            grid=(spans,),
            in_specs=[tile_block] * 8 + [token_block] * 2 + [whole] * 2,
            out_specs=[token_block] * 2 + [tile_block] * 8 + [whole] * 2,
            scratch_shapes=[pltpu.VMEM((width, columns), F32)] * 2,
        ),
        out_shape=[jax.ShapeDtypeStruct((spans * SPAN, columns), BF16)] * 2
        + [jax.ShapeDtypeStruct((NT, SUB, width), BF16)] * 8
        + [jax.ShapeDtypeStruct((width, columns), BF16)] * 2,
        compiler_params=pltpu.CompilerParams(vmem_limit_bytes=VMEM_LIMIT),
    )(key_length, *parts, query, upstream, w_key, w_value)


def body(
    queries_in,
    w_query,
    w_key,
    w_value,
    tiles,
    neighbour_owner,
    neighbour_slot,
    key_length,
    grad_context,
):
    width = tiles.shape[2]
    steps = range(1, SIDE)
    pair = ((2, SUB, width), BF16)
    line = ((2 * SIDE, SUB, width), BF16)
    group = ((NT, SUB, width), BF16)
    with jax.named_scope("gather"):
        cut = call(split_kernel, (neighbour_owner, neighbour_slot), (tiles,), [pair] * 8)
        row_a = [cut[0]] + [along_x(cut[k], k) for k in steps]
        row_b = [cut[SIDE]] + [along_y(cut[SIDE + k], k) for k in steps]
        line_a = jnp.concatenate(row_a, axis=0)
        line_b = jnp.concatenate(row_b, axis=0)
        all_a = [line_a] + [along_y(line_a, k) for k in steps]
        all_b = [line_b] + [along_x(line_b, k) for k in steps]
        own_a, own_b = call(compact_kernel, (neighbour_owner,), all_a + all_b, [group] * 2)
        part_a = [own_a] + [along_x(own_a, k) for k in steps]
        part_b = [own_b] + [along_y(own_b, k) for k in steps]
    query = jnp.dot(queries_in, w_query, preferred_element_type=F32).astype(BF16)
    with jax.named_scope("attend"):
        done = attend(key_length, part_a + part_b, query, grad_context, w_key, w_value)
    context, query_grad = done[:2]
    send_a, send_b = done[2:6], done[6:10]
    grad_wk, grad_wv = done[10:12]
    local_wq = jnp.dot(queries_in.T, query_grad, preferred_element_type=F32).astype(BF16)
    with jax.named_scope("weights"):
        summed = [lax.psum(g, "dp").astype(F32) for g in (local_wq, grad_wk, grad_wv)]
    with jax.named_scope("scatter"):
        back_a = [send_a[0]] + [along_x(send_a[k], -k) for k in steps]
        back_b = [send_b[0]] + [along_y(send_b[k], -k) for k in steps]
        wide = call(expand_kernel, (neighbour_owner,), back_a + back_b, [line] * 8)
        home_a = [wide[0]] + [along_y(wide[k], -k) for k in steps]
        home_b = [wide[SIDE]] + [along_x(wide[SIDE + k], -k) for k in steps]
        mine = call(owners_sum_kernel, (), home_a + home_b, [pair] * 8)
        last_a = [mine[0]] + [along_x(mine[k], -k) for k in steps]
        last_b = [mine[SIDE]] + [along_y(mine[SIDE + k], -k) for k in steps]
        (grad_tiles,) = call(
            tiles_kernel,
            (neighbour_owner, neighbour_slot),
            last_a + last_b,
            [(tiles.shape, F32)],
        )
    return (context, summed[0], summed[1], summed[2], grad_tiles)


def solution(mesh):
    in_specs = (
        P("dp", None),
        P(None, "enc"),
        P(None, "enc"),
        P(None, "enc"),
        P(("dp", "enc"), None, None),
        P("dp", None),
        P("dp", None),
        P("dp", None),
        P("dp", "enc"),
    )
    out_specs = (
        P("dp", "enc"),
        P(None, "enc"),
        P(None, "enc"),
        P(None, "enc"),
        P(("dp", "enc"), None, None),
    )
    return jax.shard_map(body, mesh=mesh, in_specs=in_specs, out_specs=out_specs, check_vma=False)
```

```python
import jax
import jax.numpy as jnp
from jax import lax
from jax.experimental import pallas as pl
from jax.experimental.pallas import tpu as pltpu
from jax.sharding import PartitionSpec as P

HD = 128
SPAN = 64
SIDE = 4
SUB = 16
NT = 16
STEP = 4
VMEM_LIMIT = 20 * 1024 * 1024
ATTEND_LIMIT = 36 * 1024 * 1024
F32 = jnp.float32
BF16 = jnp.bfloat16


def along_x(value, step):
    pairs = [(i, ((i // SIDE + step) % SIDE) * SIDE + i % SIDE) for i in range(SIDE * SIDE)]
    return lax.ppermute(value, "enc", pairs)


def along_y(value, step):
    pairs = [(i, (i // SIDE) * SIDE + (i + step) % SIDE) for i in range(SIDE * SIDE)]
    return lax.ppermute(value, "enc", pairs)


def place():
    own = lax.axis_index("enc")
    return own, lax.div(own, SIDE), lax.rem(own, SIDE)


def apart(here, there):
    return lax.rem(here - there + SIDE, SIDE)


def my_slots(owner, slot, own):
    count = jnp.int32(0)
    first = jnp.int32(0)
    second = jnp.int32(0)
    for t in range(NT):
        hit = owner[t // 2, t % 2] == own
        tile = slot[t // 2, t % 2]
        first = jnp.where(hit & (count == 0), tile, first)
        second = jnp.where(hit & (count == 1), tile, second)
        count = count + hit.astype(jnp.int32)
    return first, second


def named(owner, x, y):
    found = []
    for t in range(NT):
        o = owner[t // 2, t % 2]
        rank = jnp.int32(0)
        for e in range(t):
            rank = rank + (owner[e // 2, e % 2] == o).astype(jnp.int32)
        found.append((apart(x, lax.div(o, SIDE)), apart(y, lax.rem(o, SIDE)), rank))
    return found


def sub_row(at, base):
    return pl.ds(pl.multiple_of(base + lax.rem(at, SIDE) * SUB, SUB), SUB)


def split_kernel(owner, slot, tiles, *outs):
    own, x, y = place()
    for r, tile in enumerate(my_slots(owner, slot, own)):
        for k in range(SIDE):
            outs[k][r] = tiles[tile, sub_row(x + k, 0), :]
            outs[SIDE + k][r] = tiles[tile, sub_row(y + k, SIDE * SUB), :]


def compact_kernel(owner, *refs):
    in_a, in_b = refs[:SIDE], refs[SIDE : 2 * SIDE]
    out_a, out_b = refs[2 * SIDE :]
    _, x, y = place()
    for t, (dx, dy, rank) in enumerate(named(owner, x, y)):
        for step in range(SIDE):

            @pl.when(dy == step)
            def _(t=t, step=step, at=dx * 2 + rank):
                out_a[t] = in_a[step][at]

            @pl.when(dx == step)
            def _(t=t, step=step, at=dy * 2 + rank):
                out_b[t] = in_b[step][at]


def expand_kernel(owner, *refs):
    ins, outs = refs[: 2 * SIDE], refs[2 * SIDE :]
    out_a, out_b = outs[:SIDE], outs[SIDE:]
    _, x, y = place()
    for out in outs:
        out[...] = jnp.zeros_like(out)
    for t, (dx, dy, rank) in enumerate(named(owner, x, y)):
        total_a = sum(ref[t].astype(F32) for ref in ins[:SIDE]).astype(BF16)
        total_b = sum(ref[t].astype(F32) for ref in ins[SIDE:]).astype(BF16)
        for step in range(SIDE):

            @pl.when(dy == step)
            def _(step=step, at=dx * 2 + rank, total=total_a):
                out_a[step][at] = total

            @pl.when(dx == step)
            def _(step=step, at=dy * 2 + rank, total=total_b):
                out_b[step][at] = total


def owners_sum_kernel(*refs):
    in_a, in_b = refs[:SIDE], refs[SIDE : 2 * SIDE]
    out_a, out_b = refs[2 * SIDE : 3 * SIDE], refs[3 * SIDE :]
    for ins, outs in ((in_a, out_a), (in_b, out_b)):
        for k in range(SIDE):
            for r in range(2):
                outs[k][r] = sum(ref[k * 2 + r].astype(F32) for ref in ins).astype(BF16)


def tiles_kernel(owner, slot, *refs):
    in_a, in_b, out = refs[:SIDE], refs[SIDE : 2 * SIDE], refs[2 * SIDE]
    own, x, y = place()
    out[...] = jnp.zeros_like(out)
    for r, tile in enumerate(my_slots(owner, slot, own)):
        for k in range(SIDE):
            out[tile, sub_row(x + k, 0), :] += in_a[k][r].astype(F32)
            out[tile, sub_row(y + k, SIDE * SUB), :] += in_b[k][r].astype(F32)


def dot(a, b, a_dim, b_dim):
    return lax.dot_general(a, b, (((a_dim,), (b_dim,)), ((), ())), preferred_element_type=F32)


def attention_kernel(length, *refs):
    ins, (q_ref, up_ref, w_ref) = refs[: 2 * SIDE], refs[2 * SIDE : 2 * SIDE + 3]
    ctx_ref, qg_ref = refs[11:13]
    outs, g_ref, acc = refs[13 : 13 + 2 * SIDE], refs[-2], refs[-1]
    step = pl.program_id(0)
    spans = q_ref.shape[0] // SPAN
    columns = q_ref.shape[1]
    heads = columns // HD
    keys = 2 * 2 * SIDE * SUB
    _, x, y = place()
    near = jnp.concatenate(
        [ref[s * 2 + j] for s in range(spans) for j in range(2) for ref in ins], axis=0
    )
    both = dot(near, w_ref[...], 1, 0).astype(BF16)

    def tokens(s):
        return slice(s * SPAN, (s + 1) * SPAN)

    def head(h):
        return slice(h * HD, (h + 1) * HD)

    def key(s, h):
        return both[s * keys : (s + 1) * keys, h * HD : (h + 1) * HD]

    def value(s, h):
        return both[s * keys : (s + 1) * keys, columns + h * HD : columns + (h + 1) * HD]

    units = [(s, h) for s in range(spans) for h in range(heads)]
    scale = 1.0 / HD**0.5
    score = [dot(q_ref[tokens(s), head(h)], key(s, h), 1, 1) for s, h in units]
    dprobs = [dot(up_ref[tokens(s), head(h)], value(s, h), 1, 1) for s, h in units]
    score = jnp.concatenate(score, axis=0) * scale
    dprobs = jnp.concatenate(dprobs, axis=0)
    row = lax.broadcasted_iota(jnp.int32, (1, keys), 1)
    lower = (row // (SIDE * SUB)) % 2
    block = (jnp.where(lower == 0, x, y) - (row // SUB) % SIDE + SIDE) % SIDE
    position = lower * (SIDE * SUB) + block * SUB + row % SUB
    visible = []
    for s in range(spans):
        span = step * spans + s
        limit = jnp.where(row < keys // 2, length[span, 0], length[span, 1])
        visible.append(jnp.broadcast_to(position < limit, (heads * SPAN, keys)))
    visible = jnp.concatenate(visible, axis=0)
    weights = jnp.where(visible, jnp.exp(score), 0.0)
    attention = weights / jnp.sum(weights, axis=-1, keepdims=True)
    attention_b = attention.astype(BF16)
    inner = jnp.sum(attention * dprobs, axis=-1, keepdims=True)
    dscore = (attention * (dprobs - inner) * scale).astype(BF16)
    grads = []
    for s in range(spans):
        key_grads, value_grads = [], []
        for h in range(heads):
            rows = tokens(s * heads + h)
            ctx_ref[tokens(s), head(h)] = dot(attention_b[rows], value(s, h), 1, 0).astype(BF16)
            qg_ref[tokens(s), head(h)] = dot(dscore[rows], key(s, h), 1, 0).astype(BF16)
            key_grads.append(dot(dscore[rows], q_ref[tokens(s), head(h)], 0, 0).astype(BF16))
            value_grads.append(dot(attention_b[rows], up_ref[tokens(s), head(h)], 0, 0).astype(BF16))
        grads.append(jnp.concatenate(key_grads + value_grads, axis=1))
    grads = jnp.concatenate(grads, axis=0)
    partial = dot(grads, w_ref[...], 1, 1).astype(BF16)
    for s in range(spans):
        for j in range(2):
            for k, out in enumerate(outs):
                low = s * keys + (j * 2 * SIDE + k) * SUB
                out[s * 2 + j] = partial[low : low + SUB]
    gain = dot(near, grads, 0, 0)

    @pl.when(step == 0)
    def _():
        acc[...] = gain

    @pl.when(step > 0)
    def _():
        acc[...] += gain

    @pl.when(step == pl.num_programs(0) - 1)
    def _():
        g_ref[0] = acc[:, :columns].astype(BF16)
        g_ref[1] = acc[:, columns:].astype(BF16)


def query_weight_kernel(rows_0, rows_1, grads, near_e, out):
    z = pl.program_id(0)
    cut = rows_0.shape[1]
    rest = near_e.shape[1] // SIDE
    at = pl.ds(pl.multiple_of(z * rest, 32), rest)
    for core, rows in enumerate((rows_0, rows_1)):
        out[0, core, :cut] = dot(rows[...], grads[...], 0, 0).astype(BF16)
        out[0, core, cut:] = near_e[core, at]


def query_weight(queries_in, query_grad, near_e):
    tokens, width = queries_in.shape
    columns = query_grad.shape[1]
    cut = width // (2 * SIDE)
    rest = near_e.shape[1] // SIDE
    return pl.pallas_call(
        query_weight_kernel,
        grid=(SIDE,),
        in_specs=[
            pl.BlockSpec((tokens, cut), lambda z: (0, z)),
            pl.BlockSpec((tokens, cut), lambda z: (0, SIDE + z)),
            pl.BlockSpec((tokens, columns), lambda z: (0, 0)),
            pl.BlockSpec(near_e.shape, lambda z: (0, 0, 0)),
        ],
        out_specs=pl.BlockSpec((1, 2, cut + rest, columns), lambda z: (z, 0, 0, 0)),
        out_shape=pltpu.HBM((SIDE, 2, cut + rest, columns), BF16),
        compiler_params=pltpu.CompilerParams(vmem_limit_bytes=VMEM_LIMIT),
    )(queries_in, queries_in, query_grad, near_e)


def weights_kernel(chunks, out_q, out_k, out_v, bring, hold, arrive, leave):
    cut = out_q.shape[0] // (2 * SIDE)
    rest = out_k.shape[0] // SIDE
    count = chunks.shape[0]
    arrivals = [
        pltpu.make_async_copy(chunks.at[slot], bring.at[slot], arrive.at[slot])
        for slot in range(count)
    ]
    for copy in arrivals:
        copy.start()
    copies = []
    for slot in range(count):
        z, core = slot // 2, slot % 2
        out_e = out_v if core else out_k
        arrivals[slot].wait()
        hold[slot] = bring[slot].astype(F32)
        copies += [
            pltpu.make_async_copy(
                hold.at[slot, pl.ds(0, cut)],
                out_q.at[pl.ds((core * SIDE + z) * cut, cut)],
                leave.at[slot, 0],
            ),
            pltpu.make_async_copy(
                hold.at[slot, pl.ds(cut, rest)], out_e.at[pl.ds(z * rest, rest)], leave.at[slot, 1]
            ),
        ]
        copies[-2].start()
        copies[-1].start()
    for copy in copies:
        copy.wait()


def weight_outputs(chunks, shapes):
    return pl.pallas_call(
        weights_kernel,
        out_shape=[jax.ShapeDtypeStruct(shape, F32) for shape in shapes],
        in_specs=[pl.BlockSpec(memory_space=pl.ANY)],
        out_specs=[pl.BlockSpec(memory_space=pl.ANY)] * 3,
        scratch_shapes=[
            pltpu.VMEM(chunks.shape, BF16),
            pltpu.VMEM(chunks.shape, F32),
            pltpu.SemaphoreType.DMA((2 * SIDE,)),
            pltpu.SemaphoreType.DMA((2 * SIDE, 2)),
        ],
        compiler_params=pltpu.CompilerParams(vmem_limit_bytes=VMEM_LIMIT),
    )(chunks)


def call(kernel, scalars, ins, outs, make=jax.ShapeDtypeStruct):
    vmem = pl.BlockSpec(memory_space=pltpu.VMEM)
    return pl.pallas_call(
        kernel,
        out_shape=[make(shape, dtype) for shape, dtype in outs],
        in_specs=[pl.BlockSpec(memory_space=pltpu.SMEM)] * len(scalars) + [vmem] * len(ins),
        out_specs=[vmem] * len(outs),
        compiler_params=pltpu.CompilerParams(vmem_limit_bytes=VMEM_LIMIT),
    )(*scalars, *ins)


def attend(key_length, parts, query, upstream, weight):
    spans = key_length.shape[0]
    width = weight.shape[0]
    columns = query.shape[1]
    tile_block = pl.BlockSpec((2 * STEP, SUB, width), lambda c, *_: (c, 0, 0))
    token_block = pl.BlockSpec((STEP * SPAN, columns), lambda c, *_: (c, 0))
    return pl.pallas_call(
        attention_kernel,
        grid_spec=pltpu.PrefetchScalarGridSpec(
            num_scalar_prefetch=1,
            grid=(spans // STEP,),
            in_specs=[tile_block] * (2 * SIDE)
            + [token_block] * 2
            + [pl.BlockSpec(weight.shape, lambda c, *_: (0, 0))],
            out_specs=[token_block] * 2
            + [tile_block] * (2 * SIDE)
            + [pl.BlockSpec((2, width, columns), lambda c, *_: (0, 0, 0))],
            scratch_shapes=[pltpu.VMEM(weight.shape, F32)],
        ),
        out_shape=[jax.ShapeDtypeStruct((spans * SPAN, columns), BF16)] * 2
        + [pltpu.HBM((NT, SUB, width), BF16)] * (2 * SIDE)
        + [jax.ShapeDtypeStruct((2, width, columns), BF16)],
        compiler_params=pltpu.CompilerParams(vmem_limit_bytes=ATTEND_LIMIT),
    )(key_length, *parts, query, upstream, weight)


def body(
    queries_in,
    w_query,
    w_key,
    w_value,
    tiles,
    neighbour_owner,
    neighbour_slot,
    key_length,
    grad_context,
):
    width = tiles.shape[2]
    steps = range(1, SIDE)
    pair = ((2, SUB, width), BF16)
    line = ((2 * SIDE, SUB, width), BF16)
    with jax.named_scope("gather"):
        cut = call(split_kernel, (neighbour_owner, neighbour_slot), (tiles,), [pair] * 8)
        row_a = [cut[0]] + [along_x(cut[k], k) for k in steps]
        row_b = [cut[SIDE]] + [along_y(cut[SIDE + k], k) for k in steps]
        line_a = jnp.concatenate(row_a, axis=0)
        line_b = jnp.concatenate(row_b, axis=0)
        all_a = [line_a] + [along_y(line_a, k) for k in steps]
        all_b = [line_b] + [along_x(line_b, k) for k in steps]
        group = ((NT, SUB, width), BF16)
        own_a, own_b = call(compact_kernel, (neighbour_owner,), all_a + all_b, [group] * 2)
        parts = [own_a] + [along_x(own_a, k) for k in steps]
        parts += [own_b] + [along_y(own_b, k) for k in steps]
    query = jnp.dot(queries_in, w_query, preferred_element_type=F32).astype(BF16)
    weight = jnp.concatenate([w_key, w_value], axis=1)
    with jax.named_scope("attend"):
        context, query_grad, *sends, near_e = attend(
            key_length, parts, query, grad_context, weight
        )
    with jax.named_scope("scatter"):
        back = [sends[0]] + [along_x(sends[k], -k) for k in steps]
        back += [sends[SIDE]] + [along_y(sends[SIDE + k], -k) for k in steps]
    with jax.named_scope("weights"):
        local = query_weight(queries_in, query_grad, near_e)
        local = local.reshape(-1, *local.shape[2:])
        share = lax.psum_scatter(local, "dp", scatter_dimension=0, tiled=True)
    with jax.named_scope("scatter"):
        wide = call(expand_kernel, (neighbour_owner,), back, [line] * 8, pltpu.HBM)
    with jax.named_scope("scatter"):
        home_a = [wide[0]] + [along_y(wide[k], -k) for k in steps]
        home_b = [wide[SIDE]] + [along_x(wide[SIDE + k], -k) for k in steps]
    share, home_a[1] = lax.optimization_barrier((share, home_a[1]))
    with jax.named_scope("weights"):
        chunks = lax.all_gather(share, "dp", tiled=True)
        chunks = pltpu.with_memory_space_constraint(chunks, pltpu.HBM)
        grads = weight_outputs(chunks, (w_query.shape, w_key.shape, w_value.shape))
    with jax.named_scope("scatter"):
        mine = call(owners_sum_kernel, (), home_a + home_b, [pair] * 8)
        last_a = [mine[0]] + [along_x(mine[k], -k) for k in steps]
        last_b = [mine[SIDE]] + [along_y(mine[SIDE + k], -k) for k in steps]
        (grad_tiles,) = call(
            tiles_kernel,
            (neighbour_owner, neighbour_slot),
            last_a + last_b,
            [(tiles.shape, F32)],
        )
    return (context, *grads, grad_tiles)


def solution(mesh):
    in_specs = (
        P("dp", None),
        P(None, "enc"),
        P(None, "enc"),
        P(None, "enc"),
        P(("dp", "enc"), None, None),
        P("dp", None),
        P("dp", None),
        P("dp", None),
        P("dp", "enc"),
    )
    out_specs = (
        P("dp", "enc"),
        P(None, "enc"),
        P(None, "enc"),
        P(None, "enc"),
        P(("dp", "enc"), None, None),
    )
    return jax.shard_map(body, mesh=mesh, in_specs=in_specs, out_specs=out_specs, check_vma=False)
```

```python
import jax
import jax.numpy as jnp
from jax import lax
from jax.experimental import pallas as pl
from jax.experimental.pallas import tpu as pltpu
from jax.sharding import PartitionSpec as P

HD = 128
SPAN = 64
SIDE = 4
SUB = 16
NT = 16
STEP = 4
VMEM_LIMIT = 20 * 1024 * 1024
ATTEND_LIMIT = 46 * 1024 * 1024
F32 = jnp.float32
BF16 = jnp.bfloat16


def along_x(value, step):
    pairs = [(i, ((i // SIDE + step) % SIDE) * SIDE + i % SIDE) for i in range(SIDE * SIDE)]
    return lax.ppermute(value, "enc", pairs)


def along_y(value, step):
    pairs = [(i, (i // SIDE) * SIDE + (i + step) % SIDE) for i in range(SIDE * SIDE)]
    return lax.ppermute(value, "enc", pairs)


def place():
    own = lax.axis_index("enc")
    return own, lax.div(own, SIDE), lax.rem(own, SIDE)


def apart(here, there):
    return lax.rem(here - there + SIDE, SIDE)


def my_slots(owner, slot, own):
    count = jnp.int32(0)
    first = jnp.int32(0)
    second = jnp.int32(0)
    for t in range(NT):
        hit = owner[t // 2, t % 2] == own
        tile = slot[t // 2, t % 2]
        first = jnp.where(hit & (count == 0), tile, first)
        second = jnp.where(hit & (count == 1), tile, second)
        count = count + hit.astype(jnp.int32)
    return first, second


def named(owner, x, y):
    found = []
    for t in range(NT):
        o = owner[t // 2, t % 2]
        rank = jnp.int32(0)
        for e in range(t):
            rank = rank + (owner[e // 2, e % 2] == o).astype(jnp.int32)
        found.append((apart(x, lax.div(o, SIDE)), apart(y, lax.rem(o, SIDE)), rank))
    return found


def sub_row(at, base):
    return pl.ds(pl.multiple_of(base + lax.rem(at, SIDE) * SUB, SUB), SUB)


def split_kernel(owner, slot, tiles, *refs):
    outs, (held, sems) = refs[: 2 * SIDE], refs[2 * SIDE :]
    own, x, y = place()
    copies = [
        pltpu.make_async_copy(tiles.at[tile], held.at[r], sems.at[r])
        for r, tile in enumerate(my_slots(owner, slot, own))
    ]
    for copy in copies:
        copy.start()
    for copy in copies:
        copy.wait()
    for r in range(2):
        for k in range(SIDE):
            outs[k][r] = held[r, sub_row(x + k, 0), :]
            outs[SIDE + k][r] = held[r, sub_row(y + k, SIDE * SUB), :]


def compact_kernel(owner, *refs):
    in_a, in_b = refs[:SIDE], refs[SIDE : 2 * SIDE]
    out_a, out_b = refs[2 * SIDE :]
    _, x, y = place()
    for t, (dx, dy, rank) in enumerate(named(owner, x, y)):
        for step in range(SIDE):

            @pl.when(dy == step)
            def _(t=t, step=step, at=dx * 2 + rank):
                out_a[t] = in_a[step][at]

            @pl.when(dx == step)
            def _(t=t, step=step, at=dy * 2 + rank):
                out_b[t] = in_b[step][at]


def expand_kernel(owner, *refs):
    ins, outs = refs[: 2 * SIDE], refs[2 * SIDE :]
    out_a, out_b = outs[:SIDE], outs[SIDE:]
    _, x, y = place()
    for out in outs:
        out[...] = jnp.zeros_like(out)
    for t, (dx, dy, rank) in enumerate(named(owner, x, y)):
        total_a = sum(ref[t].astype(F32) for ref in ins[:SIDE]).astype(BF16)
        total_b = sum(ref[t].astype(F32) for ref in ins[SIDE:]).astype(BF16)
        for step in range(SIDE):

            @pl.when(dy == step)
            def _(step=step, at=dx * 2 + rank, total=total_a):
                out_a[step][at] = total

            @pl.when(dx == step)
            def _(step=step, at=dy * 2 + rank, total=total_b):
                out_b[step][at] = total


def owners_sum_kernel(*refs):
    in_a, in_b = refs[:SIDE], refs[SIDE : 2 * SIDE]
    out_a, out_b = refs[2 * SIDE : 3 * SIDE], refs[3 * SIDE :]
    for ins, outs in ((in_a, out_a), (in_b, out_b)):
        for k in range(SIDE):
            for r in range(2):
                outs[k][r] = sum(ref[k * 2 + r].astype(F32) for ref in ins).astype(BF16)


def tiles_kernel(owner, slot, *refs):
    in_a, in_b, out = refs[:SIDE], refs[SIDE : 2 * SIDE], refs[2 * SIDE]
    own, x, y = place()
    out[...] = jnp.zeros_like(out)
    for r, tile in enumerate(my_slots(owner, slot, own)):
        for k in range(SIDE):
            out[tile, sub_row(x + k, 0), :] += in_a[k][r].astype(F32)
            out[tile, sub_row(y + k, SIDE * SUB), :] += in_b[k][r].astype(F32)


def dot(a, b, a_dim, b_dim):
    return lax.dot_general(a, b, (((a_dim,), (b_dim,)), ((), ())), preferred_element_type=F32)


def attention_kernel(length, *refs):
    ins, (q_ref, up_ref, w_ref, in_ref) = refs[: 2 * SIDE], refs[2 * SIDE : 2 * SIDE + 4]
    ctx_ref, outs = refs[12], refs[13 : 13 + 2 * SIDE]
    g_ref, acc, held_q, rows_q, ready, arrive, leave = refs[-7:]
    step = pl.program_id(0)
    tall = STEP * SPAN
    count = rows_q.shape[0] // tall

    def bring(part):
        rows = pl.ds(part * tall, tall)
        return pltpu.make_async_copy(in_ref.at[rows], rows_q.at[rows], arrive.at[part])

    @pl.when(step == 0)
    def _():
        for part in range(count):
            bring(part).start()

    spans = q_ref.shape[0] // SPAN
    columns = q_ref.shape[1]
    heads = columns // HD
    keys = 2 * 2 * SIDE * SUB
    _, x, y = place()
    near = jnp.concatenate(
        [ref[s * 2 + j] for s in range(spans) for j in range(2) for ref in ins], axis=0
    )
    both = dot(near, w_ref[...], 1, 0).astype(BF16)

    def tokens(s):
        return slice(s * SPAN, (s + 1) * SPAN)

    def head(h):
        return slice(h * HD, (h + 1) * HD)

    def key(s, h):
        return both[s * keys : (s + 1) * keys, h * HD : (h + 1) * HD]

    def value(s, h):
        return both[s * keys : (s + 1) * keys, columns + h * HD : columns + (h + 1) * HD]

    units = [(s, h) for s in range(spans) for h in range(heads)]
    scale = 1.0 / HD**0.5
    score = [dot(q_ref[tokens(s), head(h)], key(s, h), 1, 1) for s, h in units]
    dprobs = [dot(up_ref[tokens(s), head(h)], value(s, h), 1, 1) for s, h in units]
    score = jnp.concatenate(score, axis=0) * scale
    dprobs = jnp.concatenate(dprobs, axis=0)
    row = lax.broadcasted_iota(jnp.int32, (1, keys), 1)
    lower = (row // (SIDE * SUB)) % 2
    block = (jnp.where(lower == 0, x, y) - (row // SUB) % SIDE + SIDE) % SIDE
    position = lower * (SIDE * SUB) + block * SUB + row % SUB
    visible = []
    for s in range(spans):
        span = step * spans + s
        limit = jnp.where(row < keys // 2, length[span, 0], length[span, 1])
        visible.append(jnp.broadcast_to(position < limit, (heads * SPAN, keys)))
    visible = jnp.concatenate(visible, axis=0)
    weights = jnp.where(visible, jnp.exp(score), 0.0)
    attention = weights / jnp.sum(weights, axis=-1, keepdims=True)
    attention_b = attention.astype(BF16)
    inner = jnp.sum(attention * dprobs, axis=-1, keepdims=True)
    dscore = (attention * (dprobs - inner) * scale).astype(BF16)
    grads = []
    query_grads = []
    for s in range(spans):
        key_grads, value_grads, own_grads = [], [], []
        for h in range(heads):
            rows = tokens(s * heads + h)
            ctx_ref[tokens(s), head(h)] = dot(attention_b[rows], value(s, h), 1, 0).astype(BF16)
            own_grads.append(dot(dscore[rows], key(s, h), 1, 0).astype(BF16))
            key_grads.append(dot(dscore[rows], q_ref[tokens(s), head(h)], 0, 0).astype(BF16))
            value_grads.append(dot(attention_b[rows], up_ref[tokens(s), head(h)], 0, 0).astype(BF16))
        grads.append(jnp.concatenate(key_grads + value_grads, axis=1))
        query_grads.append(jnp.concatenate(own_grads, axis=1))
    query_grads = jnp.concatenate(query_grads, axis=0)
    grads = jnp.concatenate(grads, axis=0)
    partial = dot(grads, w_ref[...], 1, 1).astype(BF16)
    for s in range(spans):
        for j in range(2):
            for k, out in enumerate(outs):
                low = s * keys + (j * 2 * SIDE + k) * SUB
                out[s * 2 + j] = partial[low : low + SUB]
    gain = dot(near, grads, 0, 0)
    width = in_ref.shape[1]
    cut = width // (2 * SIDE)
    rest = gain.shape[0] // SIDE

    held_q[pl.ds(pl.multiple_of(step * tall, tall), tall)] = query_grads

    @pl.when(step == 0)
    def _():
        acc[...] = gain

    @pl.when((step > 0) & (step < pl.num_programs(0) - 1))
    def _():
        acc[...] += gain

    @pl.when(step == pl.num_programs(0) - 1)
    def _():
        total = (acc[...] + gain).astype(BF16)
        for part in range(count):
            bring(part).wait()
        copies = []
        for core in range(2):
            for z in range(SIDE):
                i = core * SIDE + z
                slot = 2 * z + core
                part = total[z * rest : (z + 1) * rest, core * columns : (core + 1) * columns]
                ready[slot, cut:] = part
                part = dot(rows_q[:, i * cut : (i + 1) * cut], held_q[...], 0, 0)
                ready[slot, :cut] = part.astype(BF16)
                copies.append(
                    pltpu.make_async_copy(ready.at[slot], g_ref.at[slot], leave.at[slot])
                )
                copies[-1].start()
        for copy in copies:
            copy.wait()


def weights_kernel(chunks, out_q, out_k, out_v, bring, hold, arrive, leave):
    cut = out_q.shape[0] // (2 * SIDE)
    rest = out_k.shape[0] // SIDE
    count = chunks.shape[0]
    arrivals = [
        pltpu.make_async_copy(chunks.at[slot], bring.at[slot], arrive.at[slot])
        for slot in range(count)
    ]
    for copy in arrivals:
        copy.start()
    copies = []
    for slot in range(count):
        z, core = slot // 2, slot % 2
        out_e = out_v if core else out_k
        arrivals[slot].wait()
        hold[slot] = bring[slot].astype(F32)
        copies += [
            pltpu.make_async_copy(
                hold.at[slot, pl.ds(0, cut)],
                out_q.at[pl.ds((core * SIDE + z) * cut, cut)],
                leave.at[slot, 0],
            ),
            pltpu.make_async_copy(
                hold.at[slot, pl.ds(cut, rest)], out_e.at[pl.ds(z * rest, rest)], leave.at[slot, 1]
            ),
        ]
        copies[-2].start()
        copies[-1].start()
    for copy in copies:
        copy.wait()


def weight_outputs(chunks, shapes):
    return pl.pallas_call(
        weights_kernel,
        out_shape=[jax.ShapeDtypeStruct(shape, F32) for shape in shapes],
        in_specs=[pl.BlockSpec(memory_space=pl.ANY)],
        out_specs=[pl.BlockSpec(memory_space=pl.ANY)] * 3,
        scratch_shapes=[
            pltpu.VMEM(chunks.shape, BF16),
            pltpu.VMEM(chunks.shape, F32),
            pltpu.SemaphoreType.DMA((2 * SIDE,)),
            pltpu.SemaphoreType.DMA((2 * SIDE, 2)),
        ],
        compiler_params=pltpu.CompilerParams(vmem_limit_bytes=VMEM_LIMIT),
    )(chunks)


def cut_tiles(owner, slot, tiles):
    width = tiles.shape[2]
    return pl.pallas_call(
        split_kernel,
        out_shape=[jax.ShapeDtypeStruct((2, SUB, width), BF16)] * (2 * SIDE),
        in_specs=[pl.BlockSpec(memory_space=pltpu.SMEM)] * 2
        + [pl.BlockSpec(memory_space=pl.ANY)],
        out_specs=[pl.BlockSpec(memory_space=pltpu.VMEM)] * (2 * SIDE),
        scratch_shapes=[
            pltpu.VMEM((2,) + tiles.shape[1:], BF16),
            pltpu.SemaphoreType.DMA((2,)),
        ],
        compiler_params=pltpu.CompilerParams(vmem_limit_bytes=VMEM_LIMIT),
    )(owner, slot, pltpu.with_memory_space_constraint(tiles, pltpu.HBM))


def call(kernel, scalars, ins, outs, kept=None):
    vmem = pl.BlockSpec(memory_space=pltpu.VMEM)
    return pl.pallas_call(
        kernel,
        out_shape=[
            jax.ShapeDtypeStruct(*out) if kept is None or i in kept else pltpu.HBM(*out)
            for i, out in enumerate(outs)
        ],
        in_specs=[pl.BlockSpec(memory_space=pltpu.SMEM)] * len(scalars) + [vmem] * len(ins),
        out_specs=[vmem] * len(outs),
        compiler_params=pltpu.CompilerParams(vmem_limit_bytes=VMEM_LIMIT),
    )(*scalars, *ins)


def attend(key_length, parts, query, upstream, weight, queries_in):
    spans = key_length.shape[0]
    width = weight.shape[0]
    columns = query.shape[1]
    depth = queries_in.shape[1]
    chunks = (2 * SIDE, depth // (2 * SIDE) + width // SIDE, columns)
    tile_block = pl.BlockSpec((2 * STEP, SUB, width), lambda c, *_: (c, 0, 0))
    token_block = pl.BlockSpec((STEP * SPAN, columns), lambda c, *_: (c, 0))
    return pl.pallas_call(
        attention_kernel,
        grid_spec=pltpu.PrefetchScalarGridSpec(
            num_scalar_prefetch=1,
            grid=(spans // STEP,),
            in_specs=[tile_block] * (2 * SIDE)
            + [token_block] * 2
            + [pl.BlockSpec(weight.shape, lambda c, *_: (0, 0))]
            + [pl.BlockSpec(memory_space=pl.ANY)],
            out_specs=[token_block]
            + [tile_block] * (2 * SIDE)
            + [pl.BlockSpec(memory_space=pl.ANY)],
            scratch_shapes=[
                pltpu.VMEM(weight.shape, F32),
                pltpu.VMEM((spans * SPAN, columns), BF16),
                pltpu.VMEM(queries_in.shape, BF16),
                pltpu.VMEM(chunks, BF16),
                pltpu.SemaphoreType.DMA((spans // STEP,)),
                pltpu.SemaphoreType.DMA((2 * SIDE,)),
            ],
        ),
        out_shape=[jax.ShapeDtypeStruct((spans * SPAN, columns), BF16)]
        + [pltpu.HBM((NT, SUB, width), BF16)] * (2 * SIDE)
        + [pltpu.HBM(chunks, BF16)],
        compiler_params=pltpu.CompilerParams(vmem_limit_bytes=ATTEND_LIMIT),
    )(key_length, *parts, query, upstream, weight, pltpu.with_memory_space_constraint(queries_in, pltpu.HBM))


def body(
    queries_in,
    w_query,
    w_key,
    w_value,
    tiles,
    neighbour_owner,
    neighbour_slot,
    key_length,
    grad_context,
):
    width = tiles.shape[2]
    steps = range(1, SIDE)
    pair = ((2, SUB, width), BF16)
    line = ((2 * SIDE, SUB, width), BF16)
    with jax.named_scope("gather"):
        cut = cut_tiles(neighbour_owner, neighbour_slot, tiles)
        row_a = [cut[0]] + [along_x(cut[k], k) for k in steps]
        row_b = [cut[SIDE]] + [along_y(cut[SIDE + k], k) for k in steps]
        line_a = jnp.concatenate(row_a, axis=0)
        line_b = jnp.concatenate(row_b, axis=0)
        all_a = [line_a] + [along_y(line_a, k) for k in steps]
        all_b = [line_b] + [along_x(line_b, k) for k in steps]
        group = ((NT, SUB, width), BF16)
        own_a, own_b = call(compact_kernel, (neighbour_owner,), all_a + all_b, [group] * 2)
        parts = [own_a] + [along_x(own_a, k) for k in steps]
        parts += [own_b] + [along_y(own_b, k) for k in steps]
    query = jnp.dot(queries_in, w_query, preferred_element_type=F32).astype(BF16)
    weight = jnp.concatenate([w_key, w_value], axis=1)
    with jax.named_scope("attend"):
        context, *sends, local = attend(
            key_length, parts, query, grad_context, weight, queries_in
        )
    with jax.named_scope("scatter"):
        back = [sends[0]] + [along_x(sends[k], -k) for k in steps]
        back += [sends[SIDE]] + [along_y(sends[SIDE + k], -k) for k in steps]
    with jax.named_scope("weights"):
        share = lax.psum_scatter(local, "dp", scatter_dimension=0, tiled=True)
    with jax.named_scope("scatter"):
        wide = call(expand_kernel, (neighbour_owner,), back, [line] * 8, (0, SIDE))
    with jax.named_scope("scatter"):
        home_a = [wide[0]] + [along_y(wide[k], -k) for k in steps]
        home_b = [wide[SIDE]] + [along_x(wide[SIDE + k], -k) for k in steps]
    share, home_a[1] = lax.optimization_barrier((share, home_a[1]))
    with jax.named_scope("weights"):
        chunks = lax.all_gather(share, "dp", tiled=True)
        chunks = pltpu.with_memory_space_constraint(chunks, pltpu.HBM)
        grads = weight_outputs(chunks, (w_query.shape, w_key.shape, w_value.shape))
    with jax.named_scope("scatter"):
        mine = call(owners_sum_kernel, (), home_a + home_b, [pair] * 8)
        last_a = [mine[0]] + [along_x(mine[k], -k) for k in steps]
        last_b = [mine[SIDE]] + [along_y(mine[SIDE + k], -k) for k in steps]
        (grad_tiles,) = call(
            tiles_kernel,
            (neighbour_owner, neighbour_slot),
            last_a + last_b,
            [(tiles.shape, F32)],
        )
    return (context, *grads, grad_tiles)


def solution(mesh):
    in_specs = (
        P("dp", None),
        P(None, "enc"),
        P(None, "enc"),
        P(None, "enc"),
        P(("dp", "enc"), None, None),
        P("dp", None),
        P("dp", None),
        P("dp", None),
        P("dp", "enc"),
    )
    out_specs = (
        P("dp", "enc"),
        P(None, "enc"),
        P(None, "enc"),
        P(None, "enc"),
        P(("dp", "enc"), None, None),
    )
    return jax.shard_map(body, mesh=mesh, in_specs=in_specs, out_specs=out_specs, check_vma=False)
```

```python
import jax
import jax.numpy as jnp
from jax import lax
from jax.experimental import pallas as pl
from jax.experimental.pallas import tpu as pltpu
from jax.sharding import PartitionSpec as P

HD = 128
SPAN = 64
SIDE = 4
SUB = 16
NT = 16
STEP = 4
VMEM_LIMIT = 20 * 1024 * 1024
ATTEND_LIMIT = 46 * 1024 * 1024
F32 = jnp.float32
BF16 = jnp.bfloat16


def along_x(value, step):
    pairs = [(i, ((i // SIDE + step) % SIDE) * SIDE + i % SIDE) for i in range(SIDE * SIDE)]
    return lax.ppermute(value, "enc", pairs)


def along_y(value, step):
    pairs = [(i, (i // SIDE) * SIDE + (i + step) % SIDE) for i in range(SIDE * SIDE)]
    return lax.ppermute(value, "enc", pairs)


def place():
    own = lax.axis_index("enc")
    return own, lax.div(own, SIDE), lax.rem(own, SIDE)


def apart(here, there):
    return lax.rem(here - there + SIDE, SIDE)


def my_slots(owner, slot, own):
    count = jnp.int32(0)
    first = jnp.int32(0)
    second = jnp.int32(0)
    for t in range(NT):
        hit = owner[t % 2, t // 2] == own
        tile = slot[t % 2, t // 2]
        first = jnp.where(hit & (count == 0), tile, first)
        second = jnp.where(hit & (count == 1), tile, second)
        count = count + hit.astype(jnp.int32)
    return first, second


def named(owner, x, y):
    found = []
    for t in range(NT):
        o = owner[t % 2, t // 2]
        rank = jnp.int32(0)
        for e in range(t):
            rank = rank + (owner[e % 2, e // 2] == o).astype(jnp.int32)
        found.append((apart(x, lax.div(o, SIDE)), apart(y, lax.rem(o, SIDE)), rank))
    return found


def sub_row(at, base):
    return pl.ds(pl.multiple_of(base + lax.rem(at, SIDE) * SUB, SUB), SUB)


def split_kernel(owner_ref, slot_ref, tiles, *refs):
    outs, (owner, slot, held, sems) = refs[: 2 * SIDE], refs[2 * SIDE :]
    copies = [
        pltpu.make_async_copy(owner_ref, owner, sems.at[0]),
        pltpu.make_async_copy(slot_ref, slot, sems.at[1]),
    ]
    for copy in copies:
        copy.start()
    for copy in copies:
        copy.wait()
    own, x, y = place()
    copies = [
        pltpu.make_async_copy(tiles.at[tile], held.at[r], sems.at[2 + r])
        for r, tile in enumerate(my_slots(owner, slot, own))
    ]
    for copy in copies:
        copy.start()
    for copy in copies:
        copy.wait()
    for r in range(2):
        for k in range(SIDE):
            outs[k][r] = held[r, sub_row(x + k, 0), :]
            outs[SIDE + k][r] = held[r, sub_row(y + k, SIDE * SUB), :]


def compact_kernel(owner, *refs):
    in_a, in_b = refs[:SIDE], refs[SIDE : 2 * SIDE]
    out_a, out_b = refs[2 * SIDE :]
    _, x, y = place()
    for t, (dx, dy, rank) in enumerate(named(owner, x, y)):
        for step in range(SIDE):

            @pl.when(dy == step)
            def _(t=t, step=step, at=dx * 2 + rank):
                out_a[t] = in_a[step][at]

            @pl.when(dx == step)
            def _(t=t, step=step, at=dy * 2 + rank):
                out_b[t] = in_b[step][at]


def expand_kernel(owner, *refs):
    ins, outs = refs[: 2 * SIDE], refs[2 * SIDE :]
    out_a, out_b = outs[:SIDE], outs[SIDE:]
    _, x, y = place()
    for out in outs:
        out[...] = jnp.zeros_like(out)
    for t, (dx, dy, rank) in enumerate(named(owner, x, y)):
        total_a = sum(ref[t].astype(F32) for ref in ins[:SIDE]).astype(BF16)
        total_b = sum(ref[t].astype(F32) for ref in ins[SIDE:]).astype(BF16)
        for step in range(SIDE):

            @pl.when(dy == step)
            def _(step=step, at=dx * 2 + rank, total=total_a):
                out_a[step][at] = total

            @pl.when(dx == step)
            def _(step=step, at=dy * 2 + rank, total=total_b):
                out_b[step][at] = total


def owners_sum_kernel(*refs):
    in_a, in_b = refs[:SIDE], refs[SIDE : 2 * SIDE]
    out_a, out_b = refs[2 * SIDE : 3 * SIDE], refs[3 * SIDE :]
    for ins, outs in ((in_a, out_a), (in_b, out_b)):
        for k in range(SIDE):
            for r in range(2):
                outs[k][r] = sum(ref[k * 2 + r].astype(F32) for ref in ins).astype(BF16)


def dot(a, b, a_dim, b_dim):
    return lax.dot_general(a, b, (((a_dim,), (b_dim,)), ((), ())), preferred_element_type=F32)


def attention_kernel(length, *refs):
    ins, (q_ref, up_ref, w_ref, in_ref) = refs[: 2 * SIDE], refs[2 * SIDE : 2 * SIDE + 4]
    ctx_ref, outs = refs[12], refs[13 : 13 + 2 * SIDE]
    g_ref, acc, held_q, rows_q, ready, arrive, leave = refs[-7:]
    step = pl.program_id(0)
    tall = STEP * SPAN
    count = rows_q.shape[0] // tall

    def bring(part):
        rows = pl.ds(part * tall, tall)
        return pltpu.make_async_copy(in_ref.at[rows], rows_q.at[rows], arrive.at[part])

    @pl.when(step == 0)
    def _():
        for part in range(count):
            bring(part).start()

    spans = q_ref.shape[0] // SPAN
    columns = q_ref.shape[1]
    heads = columns // HD
    keys = 2 * 2 * SIDE * SUB
    _, x, y = place()
    near = jnp.concatenate(
        [ref[s * 2 + j] for s in range(spans) for j in range(2) for ref in ins], axis=0
    )
    both = dot(near, w_ref[...], 1, 0).astype(BF16)

    def tokens(s):
        return slice(s * SPAN, (s + 1) * SPAN)

    def head(h):
        return slice(h * HD, (h + 1) * HD)

    def key(s, h):
        return both[s * keys : (s + 1) * keys, h * HD : (h + 1) * HD]

    def value(s, h):
        return both[s * keys : (s + 1) * keys, columns + h * HD : columns + (h + 1) * HD]

    units = [(s, h) for s in range(spans) for h in range(heads)]
    scale = 1.0 / HD**0.5
    score = [dot(q_ref[tokens(s), head(h)], key(s, h), 1, 1) for s, h in units]
    dprobs = [dot(up_ref[tokens(s), head(h)], value(s, h), 1, 1) for s, h in units]
    score = jnp.concatenate(score, axis=0) * scale
    dprobs = jnp.concatenate(dprobs, axis=0)
    row = lax.broadcasted_iota(jnp.int32, (1, keys), 1)
    lower = (row // (SIDE * SUB)) % 2
    block = (jnp.where(lower == 0, x, y) - (row // SUB) % SIDE + SIDE) % SIDE
    position = lower * (SIDE * SUB) + block * SUB + row % SUB
    visible = []
    for s in range(spans):
        span = step * spans + s
        limit = jnp.where(row < keys // 2, length[0, span], length[1, span])
        visible.append(jnp.broadcast_to(position < limit, (heads * SPAN, keys)))
    visible = jnp.concatenate(visible, axis=0)
    weights = jnp.where(visible, jnp.exp(score), 0.0)
    attention = weights / jnp.sum(weights, axis=-1, keepdims=True)
    attention_b = attention.astype(BF16)
    inner = jnp.sum(attention * dprobs, axis=-1, keepdims=True)
    dscore = (attention * (dprobs - inner) * scale).astype(BF16)
    grads = []
    query_grads = []
    for s in range(spans):
        key_grads, value_grads, own_grads = [], [], []
        for h in range(heads):
            rows = tokens(s * heads + h)
            ctx_ref[tokens(s), head(h)] = dot(attention_b[rows], value(s, h), 1, 0).astype(BF16)
            own_grads.append(dot(dscore[rows], key(s, h), 1, 0).astype(BF16))
            key_grads.append(dot(dscore[rows], q_ref[tokens(s), head(h)], 0, 0).astype(BF16))
            value_grads.append(dot(attention_b[rows], up_ref[tokens(s), head(h)], 0, 0).astype(BF16))
        grads.append(jnp.concatenate(key_grads + value_grads, axis=1))
        query_grads.append(jnp.concatenate(own_grads, axis=1))
    query_grads = jnp.concatenate(query_grads, axis=0)
    grads = jnp.concatenate(grads, axis=0)
    partial = dot(grads, w_ref[...], 1, 1).astype(BF16)
    for s in range(spans):
        for j in range(2):
            for k, out in enumerate(outs):
                low = s * keys + (j * 2 * SIDE + k) * SUB
                out[s * 2 + j] = partial[low : low + SUB]
    gain = dot(near, grads, 0, 0)
    width = in_ref.shape[1]
    cut = width // (2 * SIDE)
    rest = gain.shape[0] // SIDE

    held_q[pl.ds(pl.multiple_of(step * tall, tall), tall)] = query_grads

    @pl.when(step == 0)
    def _():
        acc[...] = gain

    @pl.when((step > 0) & (step < pl.num_programs(0) - 1))
    def _():
        acc[...] += gain

    @pl.when(step == pl.num_programs(0) - 1)
    def _():
        total = (acc[...] + gain).astype(BF16)
        for part in range(count):
            bring(part).wait()
        copies = []
        for core in range(2):
            for z in range(SIDE):
                i = core * SIDE + z
                slot = 2 * z + core
                part = total[z * rest : (z + 1) * rest, core * columns : (core + 1) * columns]
                ready[slot, cut:] = part
                part = dot(rows_q[:, i * cut : (i + 1) * cut], held_q[...], 0, 0)
                ready[slot, :cut] = part.astype(BF16)
                copies.append(
                    pltpu.make_async_copy(ready.at[slot], g_ref.at[slot], leave.at[slot])
                )
                copies[-1].start()
        for copy in copies:
            copy.wait()


def last_kernel(owner, slot, *refs):
    in_a, in_b, chunks = refs[:SIDE], refs[SIDE : 2 * SIDE], refs[2 * SIDE]
    out_q, out_k, out_v, out_t = refs[2 * SIDE + 1 : 2 * SIDE + 5]
    bring, hold, sums, arrive, leave, leave_t = refs[2 * SIDE + 5 :]
    cut = out_q.shape[0] // (2 * SIDE)
    rest = out_k.shape[0] // SIDE
    count = chunks.shape[0]
    arrivals = [
        pltpu.make_async_copy(chunks.at[i], bring.at[i], arrive.at[i]) for i in range(count)
    ]
    for copy in arrivals:
        copy.start()
    copies = []
    for i in range(count):
        z, core = i // 2, i % 2
        out_e = out_v if core else out_k
        arrivals[i].wait()
        hold[i] = bring[i].astype(F32)
        copies += [
            pltpu.make_async_copy(
                hold.at[i, pl.ds(0, cut)],
                out_q.at[pl.ds((core * SIDE + z) * cut, cut)],
                leave.at[i, 0],
            ),
            pltpu.make_async_copy(
                hold.at[i, pl.ds(cut, rest)], out_e.at[pl.ds(z * rest, rest)], leave.at[i, 1]
            ),
        ]
        copies[-2].start()
        copies[-1].start()
    own, x, y = place()
    sums[...] = jnp.zeros_like(sums)
    for r, tile in enumerate(my_slots(owner, slot, own)):
        for k in range(SIDE):
            sums[tile, sub_row(x + k, 0), :] += in_a[k][r].astype(F32)
            sums[tile, sub_row(y + k, SIDE * SUB), :] += in_b[k][r].astype(F32)
    copies.append(pltpu.make_async_copy(sums, out_t, leave_t))
    copies[-1].start()
    for copy in copies:
        copy.wait()


def last_outputs(owner, slot, lasts, chunks, shapes):
    return pl.pallas_call(
        last_kernel,
        out_shape=[jax.ShapeDtypeStruct(shape, F32) for shape in shapes],
        in_specs=[pl.BlockSpec(memory_space=pltpu.SMEM)] * 2
        + [pl.BlockSpec(memory_space=pltpu.VMEM)] * len(lasts)
        + [pl.BlockSpec(memory_space=pl.ANY)],
        out_specs=[pl.BlockSpec(memory_space=pl.ANY)] * len(shapes),
        scratch_shapes=[
            pltpu.VMEM(chunks.shape, BF16),
            pltpu.VMEM(chunks.shape, F32),
            pltpu.VMEM(shapes[-1], F32),
            pltpu.SemaphoreType.DMA((2 * SIDE,)),
            pltpu.SemaphoreType.DMA((2 * SIDE, 2)),
            pltpu.SemaphoreType.DMA,
        ],
        compiler_params=pltpu.CompilerParams(vmem_limit_bytes=VMEM_LIMIT),
    )(owner, slot, *lasts, chunks)


def cut_tiles(owner, slot, tiles):
    width = tiles.shape[2]
    return pl.pallas_call(
        split_kernel,
        out_shape=[jax.ShapeDtypeStruct((2, SUB, width), BF16)] * (2 * SIDE),
        in_specs=[pl.BlockSpec(memory_space=pl.ANY)] * 3,
        out_specs=[pl.BlockSpec(memory_space=pltpu.VMEM)] * (2 * SIDE),
        scratch_shapes=[
            pltpu.SMEM(owner.shape, jnp.int32),
            pltpu.SMEM(slot.shape, jnp.int32),
            pltpu.VMEM((2,) + tiles.shape[1:], BF16),
            pltpu.SemaphoreType.DMA((4,)),
        ],
        compiler_params=pltpu.CompilerParams(vmem_limit_bytes=VMEM_LIMIT),
    )(*(pltpu.with_memory_space_constraint(v, pltpu.HBM) for v in (owner, slot, tiles)))


def call(kernel, scalars, ins, outs, kept=None):
    vmem = pl.BlockSpec(memory_space=pltpu.VMEM)
    return pl.pallas_call(
        kernel,
        out_shape=[
            jax.ShapeDtypeStruct(*out) if kept is None or i in kept else pltpu.HBM(*out)
            for i, out in enumerate(outs)
        ],
        in_specs=[pl.BlockSpec(memory_space=pltpu.SMEM)] * len(scalars) + [vmem] * len(ins),
        out_specs=[vmem] * len(outs),
        compiler_params=pltpu.CompilerParams(vmem_limit_bytes=VMEM_LIMIT),
    )(*scalars, *ins)


def attend(key_length, parts, query, upstream, weight, queries_in):
    spans = key_length.shape[1]
    width = weight.shape[0]
    columns = query.shape[1]
    depth = queries_in.shape[1]
    chunks = (2 * SIDE, depth // (2 * SIDE) + width // SIDE, columns)
    tile_block = pl.BlockSpec((2 * STEP, SUB, width), lambda c, *_: (c, 0, 0))
    token_block = pl.BlockSpec((STEP * SPAN, columns), lambda c, *_: (c, 0))
    return pl.pallas_call(
        attention_kernel,
        grid_spec=pltpu.PrefetchScalarGridSpec(
            num_scalar_prefetch=1,
            grid=(spans // STEP,),
            in_specs=[tile_block] * (2 * SIDE)
            + [token_block] * 2
            + [pl.BlockSpec(weight.shape, lambda c, *_: (0, 0))]
            + [pl.BlockSpec(memory_space=pl.ANY)],
            out_specs=[token_block]
            + [tile_block] * (2 * SIDE)
            + [pl.BlockSpec(memory_space=pl.ANY)],
            scratch_shapes=[
                pltpu.VMEM(weight.shape, F32),
                pltpu.VMEM((spans * SPAN, columns), BF16),
                pltpu.VMEM(queries_in.shape, BF16),
                pltpu.VMEM(chunks, BF16),
                pltpu.SemaphoreType.DMA((spans // STEP,)),
                pltpu.SemaphoreType.DMA((2 * SIDE,)),
            ],
        ),
        out_shape=[jax.ShapeDtypeStruct((spans * SPAN, columns), BF16)]
        + [pltpu.HBM((NT, SUB, width), BF16)] * (2 * SIDE)
        + [pltpu.HBM(chunks, BF16)],
        compiler_params=pltpu.CompilerParams(vmem_limit_bytes=ATTEND_LIMIT),
    )(key_length, *parts, query, upstream, weight, pltpu.with_memory_space_constraint(queries_in, pltpu.HBM))


def body(
    queries_in,
    w_query,
    w_key,
    w_value,
    tiles,
    neighbour_owner,
    neighbour_slot,
    key_length,
    grad_context,
):
    width = tiles.shape[2]
    steps = range(1, SIDE)
    neighbour_owner, neighbour_slot, key_length = (
        value.T for value in (neighbour_owner, neighbour_slot, key_length)
    )
    pair = ((2, SUB, width), BF16)
    line = ((2 * SIDE, SUB, width), BF16)
    with jax.named_scope("gather"):
        cut = cut_tiles(neighbour_owner, neighbour_slot, tiles)
        row_a = [cut[0]] + [along_x(cut[k], k) for k in steps]
        row_b = [cut[SIDE]] + [along_y(cut[SIDE + k], k) for k in steps]
        line_a = jnp.concatenate(row_a, axis=0)
        line_b = jnp.concatenate(row_b, axis=0)
        all_a = [line_a] + [along_y(line_a, k) for k in steps]
        all_b = [line_b] + [along_x(line_b, k) for k in steps]
        group = ((NT, SUB, width), BF16)
        own_a, own_b = call(compact_kernel, (neighbour_owner,), all_a + all_b, [group] * 2)
        parts = [own_a] + [along_x(own_a, k) for k in steps]
        parts += [own_b] + [along_y(own_b, k) for k in steps]
    query = jnp.dot(queries_in, w_query, preferred_element_type=F32).astype(BF16)
    weight = jnp.concatenate([w_key, w_value], axis=1)
    with jax.named_scope("attend"):
        context, *sends, local = attend(
            key_length, parts, query, grad_context, weight, queries_in
        )
    with jax.named_scope("scatter"):
        back = [sends[0]] + [along_x(sends[k], -k) for k in steps]
        back += [sends[SIDE]] + [along_y(sends[SIDE + k], -k) for k in steps]
    with jax.named_scope("weights"):
        share = lax.psum_scatter(local, "dp", scatter_dimension=0, tiled=True)
    with jax.named_scope("scatter"):
        wide = call(expand_kernel, (neighbour_owner,), back, [line] * 8, (0, SIDE))
    with jax.named_scope("scatter"):
        home_a = [wide[0]] + [along_y(wide[k], -k) for k in steps]
        home_b = [wide[SIDE]] + [along_x(wide[SIDE + k], -k) for k in steps]
    share, home_a[1] = lax.optimization_barrier((share, home_a[1]))
    with jax.named_scope("weights"):
        chunks = lax.all_gather(share, "dp", tiled=True)
        chunks = pltpu.with_memory_space_constraint(chunks, pltpu.HBM)
    with jax.named_scope("scatter"):
        mine = call(owners_sum_kernel, (), home_a + home_b, [pair] * 8)
        last_a = [mine[0]] + [along_x(mine[k], -k) for k in steps]
        last_b = [mine[SIDE]] + [along_y(mine[SIDE + k], -k) for k in steps]
        outs = last_outputs(
            neighbour_owner,
            neighbour_slot,
            last_a + last_b,
            chunks,
            (w_query.shape, w_key.shape, w_value.shape, tiles.shape),
        )
    return (context, *outs)


def solution(mesh):
    in_specs = (
        P("dp", None),
        P(None, "enc"),
        P(None, "enc"),
        P(None, "enc"),
        P(("dp", "enc"), None, None),
        P("dp", None),
        P("dp", None),
        P("dp", None),
        P("dp", "enc"),
    )
    out_specs = (
        P("dp", "enc"),
        P(None, "enc"),
        P(None, "enc"),
        P(None, "enc"),
        P(("dp", "enc"), None, None),
    )
    return jax.shard_map(body, mesh=mesh, in_specs=in_specs, out_specs=out_specs, check_vma=False)
```

```python
import jax
import jax.numpy as jnp
from jax import lax
from jax.experimental import pallas as pl
from jax.experimental.pallas import tpu as pltpu
from jax.sharding import PartitionSpec as P

HD = 128
SPAN = 64
SIDE = 4
SUB = 16
NT = 16
STEP = 4
VMEM_LIMIT = 20 * 1024 * 1024
ATTEND_LIMIT = 46 * 1024 * 1024
F32 = jnp.float32
BF16 = jnp.bfloat16


def along_x(value, step):
    pairs = [(i, ((i // SIDE + step) % SIDE) * SIDE + i % SIDE) for i in range(SIDE * SIDE)]
    return lax.ppermute(value, "enc", pairs)


def along_y(value, step):
    pairs = [(i, (i // SIDE) * SIDE + (i + step) % SIDE) for i in range(SIDE * SIDE)]
    return lax.ppermute(value, "enc", pairs)


def place():
    own = lax.axis_index("enc")
    return own, lax.div(own, SIDE), lax.rem(own, SIDE)


def apart(here, there):
    return lax.rem(here - there + SIDE, SIDE)


def my_slots(owner, slot, own):
    count = jnp.int32(0)
    first = jnp.int32(0)
    second = jnp.int32(0)
    for t in range(NT):
        hit = owner[t % 2, t // 2] == own
        tile = slot[t % 2, t // 2]
        first = jnp.where(hit & (count == 0), tile, first)
        second = jnp.where(hit & (count == 1), tile, second)
        count = count + hit.astype(jnp.int32)
    return first, second


def named(owner, x, y):
    found = []
    for t in range(NT):
        o = owner[t % 2, t // 2]
        rank = jnp.int32(0)
        for e in range(t):
            rank = rank + (owner[e % 2, e // 2] == o).astype(jnp.int32)
        found.append((apart(x, lax.div(o, SIDE)), apart(y, lax.rem(o, SIDE)), rank))
    return found


def sub_row(at, base):
    return pl.ds(pl.multiple_of(base + lax.rem(at, SIDE) * SUB, SUB), SUB)


def split_kernel(owner_ref, slot_ref, tiles, *refs):
    outs, (owner, slot, held, sems) = refs[: 2 * SIDE], refs[2 * SIDE :]
    copies = [
        pltpu.make_async_copy(owner_ref, owner, sems.at[0]),
        pltpu.make_async_copy(slot_ref, slot, sems.at[1]),
    ]
    for copy in copies:
        copy.start()
    for copy in copies:
        copy.wait()
    own, x, y = place()
    copies = [
        pltpu.make_async_copy(tiles.at[tile], held.at[r], sems.at[2 + r])
        for r, tile in enumerate(my_slots(owner, slot, own))
    ]
    for copy in copies:
        copy.start()
    for copy in copies:
        copy.wait()
    for r in range(2):
        for k in range(SIDE):
            outs[k][r] = held[r, sub_row(x + k, 0), :]
            outs[SIDE + k][r] = held[r, sub_row(y + k, SIDE * SUB), :]


def compact_kernel(owner, *refs):
    in_a, in_b = refs[:SIDE], refs[SIDE : 2 * SIDE]
    out_a, out_b = refs[2 * SIDE :]
    _, x, y = place()
    for t, (dx, dy, rank) in enumerate(named(owner, x, y)):
        for step in range(SIDE):

            @pl.when(dy == step)
            def _(t=t, step=step, at=dx * 2 + rank):
                out_a[t] = in_a[step][at]

            @pl.when(dx == step)
            def _(t=t, step=step, at=dy * 2 + rank):
                out_b[t] = in_b[step][at]


def expand_kernel(owner, *refs):
    ins, outs = refs[: 2 * SIDE], refs[2 * SIDE :]
    out_a, out_b = outs[:SIDE], outs[SIDE:]
    _, x, y = place()
    for out in outs:
        out[...] = jnp.zeros_like(out)
    for t, (dx, dy, rank) in enumerate(named(owner, x, y)):
        total_a = sum(ref[t].astype(F32) for ref in ins[:SIDE]).astype(BF16)
        total_b = sum(ref[t].astype(F32) for ref in ins[SIDE:]).astype(BF16)
        for step in range(SIDE):

            @pl.when(dy == step)
            def _(step=step, at=dx * 2 + rank, total=total_a):
                out_a[step][at] = total

            @pl.when(dx == step)
            def _(step=step, at=dy * 2 + rank, total=total_b):
                out_b[step][at] = total


def owners_sum_kernel(*refs):
    in_a, in_b = refs[:SIDE], refs[SIDE : 2 * SIDE]
    out_a, out_b = refs[2 * SIDE : 3 * SIDE], refs[3 * SIDE :]
    for ins, outs in ((in_a, out_a), (in_b, out_b)):
        for k in range(SIDE):
            for r in range(2):
                outs[k][r] = sum(ref[k * 2 + r].astype(F32) for ref in ins).astype(BF16)


def dot(a, b, a_dim, b_dim):
    return lax.dot_general(a, b, (((a_dim,), (b_dim,)), ((), ())), preferred_element_type=F32)


def attention_kernel(length, *refs):
    ins, (q_ref, up_ref, w_ref, in_ref) = refs[: 2 * SIDE], refs[2 * SIDE : 2 * SIDE + 4]
    ctx_ref, outs = refs[12], refs[13 : 13 + 2 * SIDE]
    g_ref, acc, held_q, rows_q, ready, arrive, leave = refs[-7:]
    step = pl.program_id(0)
    tall = STEP * SPAN
    count = rows_q.shape[0] // tall

    def bring(part):
        rows = pl.ds(part * tall, tall)
        return pltpu.make_async_copy(in_ref.at[rows], rows_q.at[rows], arrive.at[part])

    @pl.when(step == 0)
    def _():
        for part in range(count):
            bring(part).start()

    spans = q_ref.shape[0] // SPAN
    columns = q_ref.shape[1]
    heads = columns // HD
    keys = 2 * 2 * SIDE * SUB
    _, x, y = place()
    near = jnp.concatenate(
        [ref[s * 2 + j] for s in range(spans) for j in range(2) for ref in ins], axis=0
    )
    both = dot(near, w_ref[...], 1, 0).astype(BF16)

    def tokens(s):
        return slice(s * SPAN, (s + 1) * SPAN)

    def head(h):
        return slice(h * HD, (h + 1) * HD)

    def key(s, h):
        return both[s * keys : (s + 1) * keys, h * HD : (h + 1) * HD]

    def value(s, h):
        return both[s * keys : (s + 1) * keys, columns + h * HD : columns + (h + 1) * HD]

    units = [(s, h) for s in range(spans) for h in range(heads)]
    scale = 1.0 / HD**0.5
    score = [dot(q_ref[tokens(s), head(h)], key(s, h), 1, 1) for s, h in units]
    dprobs = [dot(up_ref[tokens(s), head(h)], value(s, h), 1, 1) for s, h in units]
    score = jnp.concatenate(score, axis=0) * scale
    dprobs = jnp.concatenate(dprobs, axis=0)
    row = lax.broadcasted_iota(jnp.int32, (1, keys), 1)
    lower = (row // (SIDE * SUB)) % 2
    block = (jnp.where(lower == 0, x, y) - (row // SUB) % SIDE + SIDE) % SIDE
    position = lower * (SIDE * SUB) + block * SUB + row % SUB
    visible = []
    for s in range(spans):
        span = step * spans + s
        limit = jnp.where(row < keys // 2, length[0, span], length[1, span])
        visible.append(jnp.broadcast_to(position < limit, (heads * SPAN, keys)))
    visible = jnp.concatenate(visible, axis=0)
    weights = jnp.where(visible, jnp.exp(score), 0.0)
    attention = weights / jnp.sum(weights, axis=-1, keepdims=True)
    attention_b = attention.astype(BF16)
    inner = jnp.sum(attention * dprobs, axis=-1, keepdims=True)
    dscore = (attention * (dprobs - inner) * scale).astype(BF16)
    grads = []
    query_grads = []
    for s in range(spans):
        key_grads, value_grads, own_grads = [], [], []
        for h in range(heads):
            rows = tokens(s * heads + h)
            ctx_ref[tokens(s), head(h)] = dot(attention_b[rows], value(s, h), 1, 0).astype(BF16)
            own_grads.append(dot(dscore[rows], key(s, h), 1, 0).astype(BF16))
            key_grads.append(dot(dscore[rows], q_ref[tokens(s), head(h)], 0, 0).astype(BF16))
            value_grads.append(dot(attention_b[rows], up_ref[tokens(s), head(h)], 0, 0).astype(BF16))
        grads.append(jnp.concatenate(key_grads + value_grads, axis=1))
        query_grads.append(jnp.concatenate(own_grads, axis=1))
    query_grads = jnp.concatenate(query_grads, axis=0)
    grads = jnp.concatenate(grads, axis=0)
    partial = dot(grads, w_ref[...], 1, 1).astype(BF16)
    for s in range(spans):
        for j in range(2):
            for k, out in enumerate(outs):
                low = s * keys + (j * 2 * SIDE + k) * SUB
                out[s * 2 + j] = partial[low : low + SUB]
    gain = dot(near, grads, 0, 0)
    width = in_ref.shape[1]
    cut = width // (2 * SIDE)
    rest = gain.shape[0] // SIDE

    held_q[pl.ds(pl.multiple_of(step * tall, tall), tall)] = query_grads

    @pl.when(step == 0)
    def _():
        acc[...] = gain

    @pl.when((step > 0) & (step < pl.num_programs(0) - 1))
    def _():
        acc[...] += gain

    @pl.when(step == pl.num_programs(0) - 1)
    def _():
        total = (acc[...] + gain).astype(BF16)
        for part in range(count):
            bring(part).wait()
        copies = []
        for core in range(2):
            for z in range(SIDE):
                i = core * SIDE + z
                slot = 2 * z + core
                part = total[z * rest : (z + 1) * rest, core * columns : (core + 1) * columns]
                ready[slot, cut:] = part
                part = dot(rows_q[:, i * cut : (i + 1) * cut], held_q[...], 0, 0)
                ready[slot, :cut] = part.astype(BF16)
                copies.append(
                    pltpu.make_async_copy(ready.at[slot], g_ref.at[slot], leave.at[slot])
                )
                copies[-1].start()
        for copy in copies:
            copy.wait()


def last_kernel(owner, slot, *refs):
    in_a, in_b, chunks = refs[:SIDE], refs[SIDE : 2 * SIDE], refs[2 * SIDE]
    out_q, out_k, out_v, out_t = refs[2 * SIDE + 1 : 2 * SIDE + 5]
    bring, hold, sums, arrive, leave, leave_t = refs[2 * SIDE + 5 :]
    cut = out_q.shape[0] // (2 * SIDE)
    rest = out_k.shape[0] // SIDE
    count = chunks.shape[0]
    arrivals = [
        pltpu.make_async_copy(chunks.at[i], bring.at[i], arrive.at[i]) for i in range(count)
    ]
    for copy in arrivals:
        copy.start()
    copies = []
    own, x, y = place()
    sums[...] = jnp.zeros_like(sums)
    for r, tile in enumerate(my_slots(owner, slot, own)):
        for k in range(SIDE):
            sums[tile, sub_row(x + k, 0), :] += in_a[k][r].astype(F32)
            sums[tile, sub_row(y + k, SIDE * SUB), :] += in_b[k][r].astype(F32)
    copies.append(pltpu.make_async_copy(sums, out_t, leave_t))
    copies[-1].start()
    for i in range(count):
        z, core = i // 2, i % 2
        out_e = out_v if core else out_k
        arrivals[i].wait()
        hold[i] = bring[i].astype(F32)
        copies += [
            pltpu.make_async_copy(
                hold.at[i, pl.ds(0, cut)],
                out_q.at[pl.ds((core * SIDE + z) * cut, cut)],
                leave.at[i, 0],
            ),
            pltpu.make_async_copy(
                hold.at[i, pl.ds(cut, rest)], out_e.at[pl.ds(z * rest, rest)], leave.at[i, 1]
            ),
        ]
        copies[-2].start()
        copies[-1].start()
    for copy in copies:
        copy.wait()


def last_outputs(owner, slot, lasts, chunks, shapes):
    return pl.pallas_call(
        last_kernel,
        out_shape=[jax.ShapeDtypeStruct(shape, F32) for shape in shapes],
        in_specs=[pl.BlockSpec(memory_space=pltpu.SMEM)] * 2
        + [pl.BlockSpec(memory_space=pltpu.VMEM)] * len(lasts)
        + [pl.BlockSpec(memory_space=pl.ANY)],
        out_specs=[pl.BlockSpec(memory_space=pl.ANY)] * len(shapes),
        scratch_shapes=[
            pltpu.VMEM(chunks.shape, BF16),
            pltpu.VMEM(chunks.shape, F32),
            pltpu.VMEM(shapes[-1], F32),
            pltpu.SemaphoreType.DMA((2 * SIDE,)),
            pltpu.SemaphoreType.DMA((2 * SIDE, 2)),
            pltpu.SemaphoreType.DMA,
        ],
        compiler_params=pltpu.CompilerParams(vmem_limit_bytes=VMEM_LIMIT),
    )(owner, slot, *lasts, chunks)


def cut_tiles(owner, slot, tiles):
    width = tiles.shape[2]
    return pl.pallas_call(
        split_kernel,
        out_shape=[jax.ShapeDtypeStruct((2, SUB, width), BF16)] * (2 * SIDE),
        in_specs=[pl.BlockSpec(memory_space=pl.ANY)] * 3,
        out_specs=[pl.BlockSpec(memory_space=pltpu.VMEM)] * (2 * SIDE),
        scratch_shapes=[
            pltpu.SMEM(owner.shape, jnp.int32),
            pltpu.SMEM(slot.shape, jnp.int32),
            pltpu.VMEM((2,) + tiles.shape[1:], BF16),
            pltpu.SemaphoreType.DMA((4,)),
        ],
        compiler_params=pltpu.CompilerParams(vmem_limit_bytes=VMEM_LIMIT),
    )(*(pltpu.with_memory_space_constraint(v, pltpu.HBM) for v in (owner, slot, tiles)))


def call(kernel, scalars, ins, outs, kept=None):
    vmem = pl.BlockSpec(memory_space=pltpu.VMEM)
    return pl.pallas_call(
        kernel,
        out_shape=[
            jax.ShapeDtypeStruct(*out) if kept is None or i in kept else pltpu.HBM(*out)
            for i, out in enumerate(outs)
        ],
        in_specs=[pl.BlockSpec(memory_space=pltpu.SMEM)] * len(scalars) + [vmem] * len(ins),
        out_specs=[vmem] * len(outs),
        compiler_params=pltpu.CompilerParams(vmem_limit_bytes=VMEM_LIMIT),
    )(*scalars, *ins)


def attend(key_length, parts, query, upstream, weight, queries_in):
    spans = key_length.shape[1]
    width = weight.shape[0]
    columns = query.shape[1]
    depth = queries_in.shape[1]
    chunks = (2 * SIDE, depth // (2 * SIDE) + width // SIDE, columns)
    tile_block = pl.BlockSpec((2 * STEP, SUB, width), lambda c, *_: (c, 0, 0))
    token_block = pl.BlockSpec((STEP * SPAN, columns), lambda c, *_: (c, 0))
    return pl.pallas_call(
        attention_kernel,
        grid_spec=pltpu.PrefetchScalarGridSpec(
            num_scalar_prefetch=1,
            grid=(spans // STEP,),
            in_specs=[tile_block] * (2 * SIDE)
            + [token_block] * 2
            + [pl.BlockSpec(weight.shape, lambda c, *_: (0, 0))]
            + [pl.BlockSpec(memory_space=pl.ANY)],
            out_specs=[token_block]
            + [tile_block] * (2 * SIDE)
            + [pl.BlockSpec(memory_space=pl.ANY)],
            scratch_shapes=[
                pltpu.VMEM(weight.shape, F32),
                pltpu.VMEM((spans * SPAN, columns), BF16),
                pltpu.VMEM(queries_in.shape, BF16),
                pltpu.VMEM(chunks, BF16),
                pltpu.SemaphoreType.DMA((spans // STEP,)),
                pltpu.SemaphoreType.DMA((2 * SIDE,)),
            ],
        ),
        out_shape=[jax.ShapeDtypeStruct((spans * SPAN, columns), BF16)]
        + [pltpu.HBM((NT, SUB, width), BF16)] * (2 * SIDE)
        + [pltpu.HBM(chunks, BF16)],
        compiler_params=pltpu.CompilerParams(vmem_limit_bytes=ATTEND_LIMIT),
    )(key_length, *parts, query, upstream, weight, pltpu.with_memory_space_constraint(queries_in, pltpu.HBM))


def body(
    queries_in,
    w_query,
    w_key,
    w_value,
    tiles,
    neighbour_owner,
    neighbour_slot,
    key_length,
    grad_context,
):
    width = tiles.shape[2]
    steps = range(1, SIDE)
    neighbour_owner, neighbour_slot, key_length = (
        value.T for value in (neighbour_owner, neighbour_slot, key_length)
    )
    pair = ((2, SUB, width), BF16)
    line = ((2 * SIDE, SUB, width), BF16)
    with jax.named_scope("gather"):
        cut = cut_tiles(neighbour_owner, neighbour_slot, tiles)
        row_a = [cut[0]] + [along_x(cut[k], k) for k in steps]
        row_b = [cut[SIDE]] + [along_y(cut[SIDE + k], k) for k in steps]
        line_a = jnp.concatenate(row_a, axis=0)
        line_b = jnp.concatenate(row_b, axis=0)
        all_a = [line_a] + [along_y(line_a, k) for k in steps]
        all_b = [line_b] + [along_x(line_b, k) for k in steps]
        group = ((NT, SUB, width), BF16)
        own_a, own_b = call(compact_kernel, (neighbour_owner,), all_a + all_b, [group] * 2)
        parts = [own_a] + [along_x(own_a, k) for k in steps]
        parts += [own_b] + [along_y(own_b, k) for k in steps]
    query = jnp.dot(queries_in, w_query, preferred_element_type=F32).astype(BF16)
    weight = jnp.concatenate([w_key, w_value], axis=1)
    with jax.named_scope("attend"):
        context, *sends, local = attend(
            key_length, parts, query, grad_context, weight, queries_in
        )
    with jax.named_scope("scatter"):
        back = [sends[0]] + [along_x(sends[k], -k) for k in steps]
        back += [sends[SIDE]] + [along_y(sends[SIDE + k], -k) for k in steps]
    with jax.named_scope("weights"):
        share = lax.psum_scatter(local, "dp", scatter_dimension=0, tiled=True)
    with jax.named_scope("scatter"):
        wide = call(expand_kernel, (neighbour_owner,), back, [line] * 8, (0, SIDE))
    with jax.named_scope("scatter"):
        home_a = [wide[0]] + [along_y(wide[k], -k) for k in steps]
        home_b = [wide[SIDE]] + [along_x(wide[SIDE + k], -k) for k in steps]
    share, home_a[1] = lax.optimization_barrier((share, home_a[1]))
    with jax.named_scope("weights"):
        chunks = lax.all_gather(share, "dp", tiled=True)
        chunks = pltpu.with_memory_space_constraint(chunks, pltpu.HBM)
    with jax.named_scope("scatter"):
        mine = call(owners_sum_kernel, (), home_a + home_b, [pair] * 8)
        last_a = [mine[0]] + [along_x(mine[k], -k) for k in steps]
        last_b = [mine[SIDE]] + [along_y(mine[SIDE + k], -k) for k in steps]
        outs = last_outputs(
            neighbour_owner,
            neighbour_slot,
            last_a + last_b,
            chunks,
            (w_query.shape, w_key.shape, w_value.shape, tiles.shape),
        )
    return (context, *outs)


def solution(mesh):
    in_specs = (
        P("dp", None),
        P(None, "enc"),
        P(None, "enc"),
        P(None, "enc"),
        P(("dp", "enc"), None, None),
        P("dp", None),
        P("dp", None),
        P("dp", None),
        P("dp", "enc"),
    )
    out_specs = (
        P("dp", "enc"),
        P(None, "enc"),
        P(None, "enc"),
        P(None, "enc"),
        P(("dp", "enc"), None, None),
    )
    return jax.shard_map(body, mesh=mesh, in_specs=in_specs, out_specs=out_specs, check_vma=False)
```
